32 devices in a mesh: tm: 8 (over z, y), pix: 2 (over x), pb: 2 (over core).
Axes of the slice: x: 2, y: 2, z: 4, core: 2. Of those that a mesh axis runs over, the one named last changes fastest.
Arguments:
- frames: bfloat16 [2, 512, 65536], P('pb', 'tm', 'pix'), may hold values from 0.05 to 15, as said below
- annulus_label: int32 [2, 65536], P('pb', 'pix'), may hold values from 0 to 3, as said below
- lag_width: int32 [2, 4], P('pb'), may hold values from 32 to 128, as said below
Outputs:
- correlation: float32 [2, 4, 512, 128], P('pb', None, 'tm', 'pix')
The draws below stay inside these ranges and needn't reach their ends.
Inputs may be any that keep to these rules, and one draw needn't show every extreme that they name: `frames`: intensities are positive. `annulus_label`: each annulus label is held by exactly 16384 pixels of every band. `lag_width`: some entry equals 128 in every draw.
All inputs are finite; a program needn't handle non-finite values.
Results may differ from the reference program's by a relative error of at most 0.0003.
Values may be sent and summed in bfloat16 or wider, within the bound.
No kernel may reach another device: no remote copies, remote signals or barrier semaphores. Data moves between devices by JAX's collectives and lax.ppermute only.
A program may use at most 64 MiB of HBM per device.

```python
import math
import jax
import jax.numpy as jnp
from jax import lax

F_DEV = 64
DELAYS_STORED = 128
PIX = 65536
RADII_IN_GROUP = 4
GROUP_NUMBER = 2
IMAGES_OVERALL = 512


def annulus_order(key):
    labels = []
    for band_index in range(GROUP_NUMBER):
        order = jax.random.permutation(jax.random.fold_in(key, 101 + band_index), PIX).astype(jnp.int32)
        labels.append(order * RADII_IN_GROUP // PIX)
    return jnp.stack(labels, axis=0).astype(jnp.int32)


def complex_noise(key):
    return jax.random.normal(key, (2, GROUP_NUMBER, PIX), jnp.float32) * math.sqrt(0.5)


def draw_frames(key, part):
    labels = annulus_order(key)
    stochastic_seeds = [jax.random.fold_in(key, 300 + offset) for offset in range(8)]
    profile = 3.0 ** (jnp.arange(PIX, dtype=jnp.float32) / (PIX - 1))
    decay_base = jnp.exp(jax.random.uniform(stochastic_seeds[0], (GROUP_NUMBER, RADII_IN_GROUP), jnp.float32, 0.0, math.log(8.0)))
    phase_shift = jax.random.uniform(stochastic_seeds[1], (GROUP_NUMBER, RADII_IN_GROUP), jnp.float32, 0.0, 2.0 * math.pi)
    frame_time = jnp.arange(IMAGES_OVERALL, dtype=jnp.float32)[:, None, None]
    relaxation_interval = decay_base * jnp.exp(0.6 * jnp.sin(2.0 * math.pi * frame_time / (4.0 * DELAYS_STORED) + phase_shift))
    flare_onset = jax.random.randint(stochastic_seeds[2], (IMAGES_OVERALL, GROUP_NUMBER, RADII_IN_GROUP), 0, DELAYS_STORED) == 0
    flare_persist = jax.random.uniform(stochastic_seeds[3], (IMAGES_OVERALL, GROUP_NUMBER, RADII_IN_GROUP), jnp.float32, 0.45, 0.9)
    inherited_speed = jnp.exp(-1.0 / relaxation_interval) * jnp.where(flare_onset, flare_persist, 1.0)
    background = 0.4
    frame_scale = jnp.ones((IMAGES_OVERALL, GROUP_NUMBER, 1), jnp.float32)
    field_start = complex_noise(stochastic_seeds[6])

    def advance(speckle, inputs):
        frame_index, rate_now, scale_now = inputs
        rate_pixel = jnp.take_along_axis(rate_now, labels, axis=1)
        fresh = complex_noise(jax.random.fold_in(stochastic_seeds[7], frame_index))
        speckle = rate_pixel * speckle + jnp.sqrt(1.0 - rate_pixel * rate_pixel) * fresh
        observed = speckle
        speckle_power = jnp.minimum(observed[0] * observed[0] + observed[1] * observed[1], 6.0)
        intensity = profile * (background + (1.0 - background) * speckle_power) * scale_now
        return (speckle, intensity.astype(jnp.bfloat16))
    final_field, stacked = lax.scan(advance, field_start, (jnp.arange(IMAGES_OVERALL, dtype=jnp.int32), inherited_speed, frame_scale))
    return jnp.transpose(stacked, (1, 0, 2))


def draw_annulus_label(key, part):
    return annulus_order(key)


def draw_lag_width(key, part):
    key_width, key_pick = jax.random.split(jax.random.fold_in(key, 7))
    widths = jax.random.randint(key_width, (GROUP_NUMBER * RADII_IN_GROUP,), DELAYS_STORED // 4, DELAYS_STORED + 1).astype(jnp.int32)
    picked = jax.random.randint(key_pick, (), 0, GROUP_NUMBER * RADII_IN_GROUP).astype(jnp.int32)
    widths = jnp.where(jnp.arange(GROUP_NUMBER * RADII_IN_GROUP, dtype=jnp.int32) == picked, DELAYS_STORED, widths)
    return widths.reshape(GROUP_NUMBER, RADII_IN_GROUP).astype(jnp.int32)


def setup_inputs(seed: int = 0) -> dict:
    keys = jax.random.split(jax.random.key(seed), 4)
    return {
        "frames": draw_frames(jax.random.fold_in(keys[3], 71), 0),
        "annulus_label": draw_annulus_label(jax.random.fold_in(keys[3], 71), 0),
        "lag_width": draw_lag_width(jax.random.fold_in(keys[3], 71), 0),
    }


def reference(frames, annulus_label, lag_width):
    band_count, frame_total, pixel_count = frames.shape
    labels = jnp.arange(RADII_IN_GROUP, dtype=jnp.int32)
    onehot = (annulus_label[:, None, :] == labels[None, :, None]).astype(jnp.float32)
    padded = jnp.concatenate([frames, jnp.zeros((band_count, DELAYS_STORED, pixel_count), frames.dtype)], axis=1)
    row_ids = jnp.arange(F_DEV, dtype=jnp.int32)[:, None]
    lag_ids = jnp.arange(DELAYS_STORED, dtype=jnp.int32)[None, :]
    annulus_size = PIX // RADII_IN_GROUP

    def one_block(step):
        start = (step * F_DEV).astype(jnp.int32)
        own_rows = lax.dynamic_slice_in_dim(frames, start, F_DEV, 1).astype(jnp.float32)
        columns = lax.dynamic_slice_in_dim(padded, start, F_DEV + DELAYS_STORED, 1).astype(jnp.float32)
        masked = own_rows[:, None, :, :] * onehot[:, :, None, :]
        tile_full = jnp.einsum("brtp,bsp->brts", masked, columns)
        banded = tile_full[:, :, row_ids, row_ids + lag_ids]
        col_sums = jnp.einsum("brp,bsp->brs", onehot, columns)
        own_sums = col_sums[:, :, :F_DEV][..., None]
        far_sums = col_sums[:, :, row_ids + lag_ids]
        global_rows = start + row_ids
        valid = (lag_ids[None, None] < lag_width[:, :, None, None]) & ((global_rows + lag_ids) < frame_total)[None, None]
        denominator = jnp.where(valid, own_sums * far_sums, 1.0)
        return jnp.where(valid, annulus_size * banded / denominator, 0.0)

    blocks = lax.map(one_block, jnp.arange(frame_total // F_DEV, dtype=jnp.int32))
    return blocks.transpose(1, 2, 0, 3, 4).reshape(band_count, RADII_IN_GROUP, frame_total, DELAYS_STORED)
```

```python
import functools

import jax
import jax.numpy as jnp
from jax import lax
from jax.experimental import pallas as pl
from jax.experimental.pallas import tpu as pltpu
from jax.sharding import PartitionSpec as P

DELAYS_STORED = 128
PIX = 65536
RADII = 4
ROWS = 64
UNITS = 16
PIECES = ((0, 8), (8, 6), (14, 2))
NT = (((1,), (1,)), ((), ()))


def packed(tile):
    half = tile.shape[0] // 2
    return jnp.concatenate([tile[:half], tile[half:]], axis=1)


def masked_by_annulus(block, label):
    return [block * (label == a).astype(block.dtype) for a in range(RADII)]


def sums_of(label, columns):
    ids = lax.broadcasted_iota(jnp.int32, (8, label.shape[1]), 0)
    onehot = (label == ids).astype(jnp.float32).astype(columns.dtype)
    return lax.dot_general(onehot, columns, NT, preferred_element_type=jnp.float32)


def own_kernel(steps, frames_ref, label_ref, out_ref, acc, acc_sums):
    step = pl.program_id(0)

    @pl.when(step == 0)
    def _():
        acc[...] = jnp.zeros_like(acc)
        acc_sums[...] = jnp.zeros_like(acc_sums)

    block = frames_ref[0]
    label = label_ref[...]
    rows = jnp.concatenate(masked_by_annulus(block, label), axis=0)
    acc[...] += lax.dot_general(rows, block, NT, preferred_element_type=jnp.float32)
    acc_sums[...] += sums_of(label, block)

    @pl.when(step == steps - 1)
    def _():
        tile = acc[...]
        t = lax.rem(lax.broadcasted_iota(jnp.int32, tile.shape, 0), ROWS)
        below = lax.broadcasted_iota(jnp.int32, tile.shape, 1) < t
        out_ref[: 2 * ROWS] = packed(jnp.where(below, 0.0, tile))
        sums = acc_sums[...]
        out_ref[2 * ROWS :] = jnp.concatenate([sums, sums], axis=1)


def cost(pixels, rows, columns):
    return pl.CostEstimate(
        flops=2 * rows * columns * pixels, bytes_accessed=2 * columns * pixels, transcendentals=0
    )


def own_part(frames, label):
    pixels = frames.shape[2]
    width = pixels // 8
    steps = pixels // width
    shape = (2 * ROWS + 8, 128)
    return pl.pallas_call(
        functools.partial(own_kernel, steps),
        grid=(steps,),
        in_specs=[
            pl.BlockSpec((1, ROWS, width), lambda k: (0, 0, k)),
            pl.BlockSpec((1, width), lambda k: (0, k)),
        ],
        out_specs=pl.BlockSpec(shape, lambda k: (0, 0)),
        out_shape=jax.ShapeDtypeStruct(shape, jnp.float32),
        scratch_shapes=[
            pltpu.VMEM((RADII * ROWS, ROWS), jnp.float32),
            pltpu.VMEM((8, ROWS), jnp.float32),
        ],
        compiler_params=pltpu.CompilerParams(vmem_limit_bytes=16 << 20),
        cost_estimate=cost(pixels, 512, 256),
        name="own_tile_and_sums",
    )(frames, label)


def chunk_kernel(steps, first, last, place_ref, own_ref, label_ref, near_ref, far_ref, *refs):
    if not first:
        before_ref, before_sums_ref, *refs = refs
    *out_refs, acc, acc_sums = refs
    step = pl.program_id(0)

    @pl.when(step == 0)
    def _():
        acc[...] = jnp.zeros_like(acc) if first else before_ref[...]
        acc_sums[...] = jnp.zeros_like(acc_sums) if first else before_sums_ref[...]

    later = place_ref[0] == 1
    own, near, far = own_ref[0], near_ref[0], far_ref[0]
    earliest = jnp.where(later, far, own)
    latest = jnp.where(later, own, far)
    label = label_ref[...]
    rows = jnp.concatenate(masked_by_annulus(earliest, label) + masked_by_annulus(near, label), axis=0)
    columns = jnp.concatenate([near, latest], axis=0)
    acc[...] += lax.dot_general(rows, columns, NT, preferred_element_type=jnp.float32)
    acc_sums[...] += sums_of(label, columns)

    @pl.when(step == steps - 1)
    def _():
        if not last:
            out_refs[0][...] = acc[...]
            out_refs[1][...] = acc_sums[...]
            return
        half = RADII * ROWS
        shape = (half, ROWS)
        t = lax.rem(lax.broadcasted_iota(jnp.int32, shape, 0), ROWS)
        below = lax.broadcasted_iota(jnp.int32, shape, 1) < t
        near_tile = acc[:half, :ROWS]
        far_tile = acc[:half, ROWS:]
        next_tile = acc[half:, ROWS:]
        second = place_ref[1] == 1
        here = (jnp.where(below, near_tile, 0.0), jnp.where(below, far_tile, near_tile))
        after = (jnp.where(below, next_tile, 0.0), jnp.where(below, 0.0, next_tile))
        sums = acc_sums[...]
        lane = lax.broadcasted_iota(jnp.int32, sums.shape, 1)
        after_sums = jnp.where(lane < ROWS, pltpu.roll(sums, ROWS, 1), 0.0)
        for k, ((low, high), row) in enumerate(((here, sums), (after, after_sums))):
            out_refs[2 * k][: 2 * ROWS] = packed(jnp.where(second, high, low))
            out_refs[2 * k + 1][: 2 * ROWS] = packed(jnp.where(second, low, high))
            out_refs[2 * k][2 * ROWS :] = row
            out_refs[2 * k + 1][2 * ROWS :] = row


def chunk_part(place, piece, label, start, near, far, before, last):
    size = near.shape[2]
    width = size // max(1, size // (label.shape[1] // 8))
    steps, offset = size // width, start // width
    acc_shape, sums_shape = (2 * RADII * ROWS, 2 * ROWS), (8, 2 * ROWS)
    message = (2 * ROWS + 8, 2 * ROWS)

    def whole(shape):
        return pl.BlockSpec(shape, lambda k: (0, 0))

    block = pl.BlockSpec((1, ROWS, width), lambda k: (0, 0, k))
    in_specs = [
        pl.BlockSpec(memory_space=pltpu.SMEM),
        block,
        pl.BlockSpec((1, width), lambda k: (0, k + offset)),
        block,
        block,
    ]
    operands = [place, piece, label, near, far]
    if before is not None:
        in_specs += [whole(acc_shape), whole(sums_shape)]
        operands += before
    shapes = [message] * 4 if last else [acc_shape, sums_shape]
    return pl.pallas_call(
        functools.partial(chunk_kernel, steps, before is None, last),
        grid=(steps,),
        in_specs=in_specs,
        out_specs=[whole(shape) for shape in shapes],
        out_shape=[jax.ShapeDtypeStruct(shape, jnp.float32) for shape in shapes],
        scratch_shapes=[pltpu.VMEM(acc_shape, jnp.float32), pltpu.VMEM(sums_shape, jnp.float32)],
        compiler_params=pltpu.CompilerParams(vmem_limit_bytes=16 << 20),
        cost_estimate=cost(size, 1024, 256),
        name="chunk_tiles",
    )(*operands)


def final_kernel(place_ref, factor_ref, own_ref, kept_ref, *refs):
    *message_refs, out_ref = refs
    total = jnp.where(place_ref[0] == 0, kept_ref[...], 0.0)
    for ref in message_refs:
        total = total + ref[...]
    own = own_ref[...]
    first = place_ref[1] == 0
    tile = total[: 2 * ROWS] + jnp.where(first, own[: 2 * ROWS], 0.0)
    ahead, present = total[2 * ROWS :], own[2 * ROWS :]
    lane = lax.broadcasted_iota(jnp.int32, ahead.shape, 1)
    moved = pltpu.roll(ahead, ROWS, 1)
    same = jnp.where(first, present, jnp.where(lane < ROWS, ahead, moved))
    beyond = jnp.where(first == (lane < ROWS), ahead, moved)
    t = lax.rem(lax.broadcasted_iota(jnp.int32, tile.shape, 0), ROWS)
    s = lax.rem(lax.broadcasted_iota(jnp.int32, tile.shape, 1), ROWS)

    def spread(row):
        pairs = [jnp.where(lane[:1] < ROWS, row[a : a + 1], row[2 + a : 3 + a]) for a in range(2)]
        return jnp.concatenate([jnp.broadcast_to(pair, (ROWS, 2 * ROWS)) for pair in pairs], axis=0)

    far = jnp.where(s < t, spread(beyond), spread(same))
    factor = factor_ref[...]
    tile = jnp.where(factor > 0.0, tile * factor / far, 0.0)
    for group in range(2):
        part = tile[:, group * ROWS : (group + 1) * ROWS]
        twice = jnp.concatenate([part, part], axis=1)
        for bit in range(6):
            turned = pltpu.roll(twice, 128 - (1 << bit), 1)
            twice = jnp.where((t >> bit) & 1 == 1, turned, twice)
        for a in range(2):
            out_ref[0, 2 * group + a] = twice[a * ROWS : (a + 1) * ROWS, :ROWS]


def final_part(place, factor, own, kept, messages):
    vmem = pl.BlockSpec(memory_space=pltpu.VMEM)
    return pl.pallas_call(
        final_kernel,
        in_specs=[pl.BlockSpec(memory_space=pltpu.SMEM)] + [vmem] * (3 + len(messages)),
        out_specs=vmem,
        out_shape=jax.ShapeDtypeStruct((1, RADII, ROWS, ROWS), jnp.float32),
        compiler_params=pltpu.CompilerParams(vmem_limit_bytes=16 << 20),
        name="normalise_and_skew",
    )(place, factor, own, kept, *messages)


def factors(own, lag_width):
    tm, pix = lax.axis_index("tm"), lax.axis_index("pix")
    devices = lax.axis_size("tm")
    t = lax.broadcasted_iota(jnp.int32, (RADII, ROWS, ROWS), 1)
    s = lax.broadcasted_iota(jnp.int32, (RADII, ROWS, ROWS), 2)
    lag = jnp.where(s >= t, s - t, s - t + ROWS) + pix * ROWS
    valid = (lag < lag_width[0][:, None, None]) & (tm * ROWS + t + lag < devices * ROWS)
    annulus_size = PIX // RADII
    result = jnp.where(valid, annulus_size / own[:, :, None], 0.0)
    return packed(result.reshape(RADII * ROWS, ROWS))


def shards(frames, annulus_label, lag_width):
    devices = lax.axis_size("tm")
    pixels = frames.shape[2]
    pb, pix = lax.axis_index("pb"), lax.axis_index("pix")
    place = jnp.stack([pb, pix]).astype(jnp.int32)

    def far_pairs():
        for i in range(devices):
            for band, target in ((0, i - 2), (1, i + 2)):
                if 0 <= target < devices:
                    yield 2 * i + band, 2 * target + band

    def near_pairs():
        for i in range(devices):
            band, target = (0, i - 1) if i % 2 else (1, i + 1)
            if target < devices:
                yield 2 * i + band, 2 * target + band

    tm_pb = ("tm", "pb")

    def sent(piece):
        far = lax.ppermute(piece, tm_pb, list(far_pairs()))
        near = lax.ppermute(piece, tm_pb, list(near_pairs()))
        return near, far

    unit = pixels // UNITS
    pieces = [
        lax.slice_in_dim(frames, begin * unit, (begin + count) * unit, axis=2) for begin, count in PIECES
    ]
    received = []
    for index, piece in enumerate(pieces):
        if index >= 2:
            piece, _ = lax.optimization_barrier((piece, received[index - 2]))
        received.append(sent(piece))

    own = own_part(frames, annulus_label)
    own = own + lax.ppermute(own, "pix", [(0, 1), (1, 0)])
    factor = factors(own[2 * ROWS : 2 * ROWS + RADII, :ROWS], lag_width)

    state = None
    for index, ((begin, _), piece, (near, far)) in enumerate(zip(PIECES, pieces, received)):
        last = index == len(pieces) - 1
        state = chunk_part(place, piece, annulus_label, begin * unit, near, far, state, last)
    here_same, here_other, after_same, after_other = state

    def message_pairs(step, flip):
        for i in range(devices):
            for band in range(2):
                target = i + step if band == 0 else i - 2 + step
                has_near = i % 2 == band
                if not 0 <= target < devices:
                    continue
                if (step and not has_near) or (not step and not flip and band == 0):
                    continue
                for x in range(2):
                    yield (i * 2 + x) * 2 + band, (target * 2 + (x ^ flip)) * 2 + band

    everywhere = ("tm", "pix", "pb")
    messages = [
        lax.ppermute(message, everywhere, list(message_pairs(step, flip)))
        for message, step, flip in (
            (here_same, 0, 0),
            (here_other, 0, 1),
            (after_same, 1, 0),
            (after_other, 1, 1),
        )
    ]
    return final_part(place, factor, own, here_same, messages)


def solution(mesh):
    return jax.shard_map(
        shards,
        mesh=mesh,
        in_specs=(P("pb", "tm", "pix"), P("pb", "pix"), P("pb", None)),
        out_specs=P("pb", None, "tm", "pix"),
        check_vma=False,
    )
```

```python
import functools

import jax
import jax.numpy as jnp
from jax import lax
from jax.experimental import pallas as pl
from jax.experimental.pallas import tpu as pltpu
from jax.sharding import PartitionSpec as P

DELAYS_STORED = 128
PIX = 65536
RADII = 4
ROWS = 64
UNITS = 16
SIZES = (7, 5, 3, 1)
GATES = (None, None, None, None)
STRIP = 2048
NT = (((1,), (1,)), ((), ()))


def packed(tile):
    half = tile.shape[0] // 2
    return jnp.concatenate([tile[:half], tile[half:]], axis=1)


def masked_by_annulus(block, label):
    return [block * (label == a).astype(block.dtype) for a in range(RADII)]


def annulus_rows(label):
    ids = lax.broadcasted_iota(jnp.int32, (16, label.shape[1]), 0)
    return (label == ids).astype(jnp.float32).astype(jnp.bfloat16)


def products(rows, columns):
    return lax.dot_general(
        jnp.concatenate(rows, axis=0), columns, NT, preferred_element_type=jnp.float32
    )


def strips(size):
    return [(begin, min(begin + STRIP, size)) for begin in range(0, size, STRIP)]


def own_kernel(label_ref, *refs):
    *piece_refs, out_ref = refs
    half = RADII * ROWS
    total, offset = None, 0
    for piece_ref in piece_refs:
        size = piece_ref.shape[2]
        for begin, end in strips(size):
            block = piece_ref[0, :, begin:end]
            label = label_ref[:, offset + begin : offset + end]
            part = products(masked_by_annulus(block, label) + [annulus_rows(label)], block)
            total = part if total is None else total + part
        offset += size
    tile, sums = total[:half], total[half : half + 8]
    t = lax.rem(lax.broadcasted_iota(jnp.int32, tile.shape, 0), ROWS)
    below = lax.broadcasted_iota(jnp.int32, tile.shape, 1) < t
    out_ref[: 2 * ROWS] = packed(jnp.where(below, 0.0, tile))
    out_ref[2 * ROWS :] = jnp.concatenate([sums, sums], axis=1)


def cost(pixels, rows, columns):
    return pl.CostEstimate(
        flops=2 * rows * columns * pixels, bytes_accessed=2 * columns * pixels, transcendentals=0
    )


def own_part(label, pieces):
    vmem = pl.BlockSpec(memory_space=pltpu.VMEM)
    return pl.pallas_call(
        own_kernel,
        in_specs=[vmem] * (1 + len(pieces)),
        out_specs=vmem,
        out_shape=jax.ShapeDtypeStruct((2 * ROWS + 8, 2 * ROWS), jnp.float32),
        compiler_params=pltpu.CompilerParams(vmem_limit_bytes=8 << 20),
        cost_estimate=cost(label.shape[1], 512, 256),
        name="own_tile_and_sums",
    )(label, *pieces)


def chunk_kernel(start, first, last, place_ref, own_ref, label_ref, far_ref, near_ref, *refs):
    if first:
        before_ref = None
    else:
        before_ref, *refs = refs
    if last:
        *out_refs, acc = refs
    else:
        (acc,) = refs
    half = RADII * ROWS
    later = place_ref[0] == 1
    pieces = strips(near_ref.shape[2])

    def add(with_near):
        total = None
        for begin, end in pieces:
            own, near, far = (ref[0, :, begin:end] for ref in (own_ref, near_ref, far_ref))
            earliest = jnp.where(later, far, own)
            latest = jnp.where(later, own, far)
            label = label_ref[:, start + begin : start + end]
            rows = [annulus_rows(label)] + masked_by_annulus(earliest, label)
            if with_near:
                rows += masked_by_annulus(near, label)
            part = products(rows, jnp.concatenate([near, latest], axis=0))
            total = part if total is None else total + part
        count = total.shape[0]
        acc[:count] = total if first else total + before_ref[:count]
        if not with_near:
            acc[count:] = jnp.zeros_like(acc[count:])

    @pl.when(place_ref[2] == 1)
    def _():
        add(True)

    @pl.when(place_ref[2] == 0)
    def _():
        add(False)

    if not last:
        return
    shape = (half, ROWS)
    t = lax.rem(lax.broadcasted_iota(jnp.int32, shape, 0), ROWS)
    below = lax.broadcasted_iota(jnp.int32, shape, 1) < t
    near_tile = acc[16 : 16 + half, :ROWS]
    far_tile = acc[16 : 16 + half, ROWS:]
    next_tile = acc[16 + half :, ROWS:]
    second = place_ref[1] == 1
    here = (jnp.where(below, near_tile, 0.0), jnp.where(below, far_tile, near_tile))
    after = (jnp.where(below, next_tile, 0.0), jnp.where(below, 0.0, next_tile))
    sums = acc[:8]
    lane = lax.broadcasted_iota(jnp.int32, sums.shape, 1)
    beside = (lane < ROWS) & (place_ref[2] == 1)
    after_sums = jnp.where(beside, pltpu.roll(sums, ROWS, 1), 0.0)
    for k, ((low, high), row) in enumerate(((here, sums), (after, after_sums))):
        out_refs[2 * k][: 2 * ROWS] = packed(jnp.where(second, high, low))
        out_refs[2 * k + 1][: 2 * ROWS] = packed(jnp.where(second, low, high))
        out_refs[2 * k][2 * ROWS :] = row
        out_refs[2 * k + 1][2 * ROWS :] = row


def chunk_part(place, piece, label, start, near, far, before, last):
    size = near.shape[2]
    acc_shape = (16 + 2 * RADII * ROWS, 2 * ROWS)
    message = (2 * ROWS + 8, 2 * ROWS)
    vmem = pl.BlockSpec(memory_space=pltpu.VMEM)
    operands = [place, piece, label, far, near] + ([] if before is None else [before])
    shapes = [message] * 4 if last else [acc_shape]
    return pl.pallas_call(
        functools.partial(chunk_kernel, start, before is None, last),
        in_specs=[pl.BlockSpec(memory_space=pltpu.SMEM)] + [vmem] * (len(operands) - 1),
        out_specs=[vmem] * len(shapes),
        out_shape=[jax.ShapeDtypeStruct(shape, jnp.float32) for shape in shapes],
        scratch_shapes=[pltpu.VMEM(acc_shape, jnp.float32)] if last else [],
        compiler_params=pltpu.CompilerParams(vmem_limit_bytes=8 << 20),
        cost_estimate=cost(size, 1024, 256),
        name="chunk_tiles",
    )(*operands)


def final_kernel(place_ref, factor_ref, own_ref, kept_ref, *refs):
    *message_refs, out_ref = refs
    total = jnp.where(place_ref[0] == 0, kept_ref[...], 0.0)
    for ref in message_refs:
        total = total + ref[...]
    own = own_ref[...]
    first = place_ref[1] == 0
    tile = total[: 2 * ROWS] + jnp.where(first, own[: 2 * ROWS], 0.0)
    ahead, present = total[2 * ROWS :], own[2 * ROWS :]
    lane = lax.broadcasted_iota(jnp.int32, ahead.shape, 1)
    moved = pltpu.roll(ahead, ROWS, 1)
    same = jnp.where(first, present, jnp.where(lane < ROWS, ahead, moved))
    beyond = jnp.where(first == (lane < ROWS), ahead, moved)
    t = lax.rem(lax.broadcasted_iota(jnp.int32, tile.shape, 0), ROWS)
    s = lax.rem(lax.broadcasted_iota(jnp.int32, tile.shape, 1), ROWS)

    def spread(row):
        pairs = [jnp.where(lane[:1] < ROWS, row[a : a + 1], row[2 + a : 3 + a]) for a in range(2)]
        return jnp.concatenate([jnp.broadcast_to(pair, (ROWS, 2 * ROWS)) for pair in pairs], axis=0)

    far = jnp.where(s < t, spread(beyond), spread(same))
    factor = factor_ref[...]
    tile = jnp.where(factor > 0.0, tile * factor / far, 0.0)
    for group in range(2):
        part = tile[:, group * ROWS : (group + 1) * ROWS]
        twice = jnp.concatenate([part, part], axis=1)
        for bit in range(6):
            turned = pltpu.roll(twice, 128 - (1 << bit), 1)
            twice = jnp.where((t >> bit) & 1 == 1, turned, twice)
        for a in range(2):
            out_ref[0, 2 * group + a] = twice[a * ROWS : (a + 1) * ROWS, :ROWS]


def final_part(place, factor, own, kept, messages):
    vmem = pl.BlockSpec(memory_space=pltpu.VMEM)
    return pl.pallas_call(
        final_kernel,
        in_specs=[pl.BlockSpec(memory_space=pltpu.SMEM)] + [vmem] * (3 + len(messages)),
        out_specs=vmem,
        out_shape=jax.ShapeDtypeStruct((1, RADII, ROWS, ROWS), jnp.float32),
        compiler_params=pltpu.CompilerParams(vmem_limit_bytes=8 << 20),
        name="normalise_and_skew",
    )(place, factor, own, kept, *messages)


def factors(own, lag_width):
    tm, pix = lax.axis_index("tm"), lax.axis_index("pix")
    devices = lax.axis_size("tm")
    t = lax.broadcasted_iota(jnp.int32, (RADII, ROWS, ROWS), 1)
    s = lax.broadcasted_iota(jnp.int32, (RADII, ROWS, ROWS), 2)
    lag = jnp.where(s >= t, s - t, s - t + ROWS) + pix * ROWS
    valid = (lag < lag_width[0][:, None, None]) & (tm * ROWS + t + lag < devices * ROWS)
    annulus_size = PIX // RADII
    result = jnp.where(valid, annulus_size / own[:, :, None], 0.0)
    return packed(result.reshape(RADII * ROWS, ROWS))


def shards(frames, annulus_label, lag_width):
    devices = lax.axis_size("tm")
    pixels = frames.shape[2]
    pb, pix = lax.axis_index("pb"), lax.axis_index("pix")
    has_near = (lax.axis_index("tm") % 2 == pb)
    place = jnp.stack([pb, pix, has_near.astype(jnp.int32)]).astype(jnp.int32)

    def far_pairs():
        for i in range(devices):
            for band, target in ((0, i - 2), (1, i + 2)):
                if 0 <= target < devices:
                    yield 2 * i + band, 2 * target + band

    def near_pairs():
        for i in range(devices):
            band, target = (0, i - 1) if i % 2 else (1, i + 1)
            if target < devices:
                yield 2 * i + band, 2 * target + band

    tm_pb = ("tm", "pb")

    def sent(piece):
        near = lax.ppermute(piece, tm_pb, list(near_pairs()))
        far = lax.ppermute(piece, tm_pb, list(far_pairs()))
        return near, far

    unit = pixels // UNITS
    starts = [sum(SIZES[:index]) * unit for index in range(len(SIZES))]
    pieces = [
        lax.slice_in_dim(frames, start, start + count * unit, axis=2) for start, count in zip(starts, SIZES)
    ]
    own = own_part(annulus_label, pieces)
    own = own + lax.ppermute(own, "pix", [(0, 1), (1, 0)])
    factor = factors(own[2 * ROWS : 2 * ROWS + RADII, :ROWS], lag_width)

    received, states, sendable = {}, [], list(pieces)

    def send(index):
        piece = pieces[index]
        if GATES[index]:
            kind, after = GATES[index]
            gate = {"done": received.get(after), "own": own, "state": states[after] if kind == "state" else None}
            piece, _ = lax.optimization_barrier((piece, gate[kind]))
        received[index] = sent(piece)

    for index in range(len(SIZES)):
        for other in range(len(SIZES)):
            gate = GATES[other]
            if other not in received and (gate is None or gate[1] < index):
                send(other)
        near, far = received[index]
        last = index == len(SIZES) - 1
        before = states[-1] if states else None
        result = chunk_part(place, pieces[index], annulus_label, starts[index], near, far, before, last)
        states.append(result if last else result[0])
    state = states[-1]
    here_same, here_other, after_same, after_other = state

    def message_pairs(step, flip):
        for i in range(devices):
            for band in range(2):
                target = i ^ 1 if step else (i if band == 0 else i - 2)
                if not 0 <= target < devices or not (step or flip or band):
                    continue
                for x in range(2):
                    yield (i * 2 + x) * 2 + band, (target * 2 + (x ^ flip)) * 2 + band

    everywhere = ("tm", "pix", "pb")
    messages = [
        lax.ppermute(message, everywhere, list(message_pairs(step, flip)))
        for message, step, flip in (
            (here_same, 0, 0),
            (here_other, 0, 1),
            (after_same, 1, 0),
            (after_other, 1, 1),
        )
    ]
    return final_part(place, factor, own, here_same, messages)


def solution(mesh):
    return jax.shard_map(
        shards,
        mesh=mesh,
        in_specs=(P("pb", "tm", "pix"), P("pb", "pix"), P("pb", None)),
        out_specs=P("pb", None, "tm", "pix"),
        check_vma=False,
    )
```

```python
import functools

import jax
import jax.numpy as jnp
from jax import lax
from jax.experimental import pallas as pl
from jax.experimental.pallas import tpu as pltpu
from jax.sharding import PartitionSpec as P

DELAYS_STORED = 128
PIX = 65536
RADII = 4
ROWS = 64
UNITS = 16
SIZES = (7, 5, 3, 1)
GATES = (None, None, None, None)
STRIP = 2048
NT = (((1,), (1,)), ((), ()))


def place():
    band = lax.axis_index("pb")
    return band, lax.axis_index("pix") == 1, lax.rem(lax.axis_index("tm"), 2) == band


def packed(tile):
    half = tile.shape[0] // 2
    return jnp.concatenate([tile[:half], tile[half:]], axis=1)


def masked_by_annulus(block, label):
    return [block * (label == a).astype(block.dtype) for a in range(RADII)]


def annulus_rows(label):
    ids = lax.broadcasted_iota(jnp.int32, (16, label.shape[1]), 0)
    return (label == ids).astype(jnp.float32).astype(jnp.bfloat16)


def products(rows, columns):
    return lax.dot_general(
        jnp.concatenate(rows, axis=0), columns, NT, preferred_element_type=jnp.float32
    )


def strips(size):
    return [(begin, min(begin + STRIP, size)) for begin in range(0, size, STRIP)]


def own_kernel(label_ref, *refs):
    *piece_refs, out_ref = refs
    half = RADII * ROWS
    total, offset = None, 0
    for piece_ref in piece_refs:
        size = piece_ref.shape[2]
        for begin, end in strips(size):
            block = piece_ref[0, :, begin:end]
            label = label_ref[:, offset + begin : offset + end]
            part = products(masked_by_annulus(block, label) + [annulus_rows(label)], block)
            total = part if total is None else total + part
        offset += size
    tile, sums = total[:half], total[half : half + 8]
    t = lax.rem(lax.broadcasted_iota(jnp.int32, tile.shape, 0), ROWS)
    below = lax.broadcasted_iota(jnp.int32, tile.shape, 1) < t
    out_ref[: 2 * ROWS] = packed(jnp.where(below, 0.0, tile))
    out_ref[2 * ROWS :] = jnp.concatenate([sums, sums], axis=1)


def cost(pixels, rows, columns):
    return pl.CostEstimate(
        flops=2 * rows * columns * pixels, bytes_accessed=2 * columns * pixels, transcendentals=0
    )


def own_part(label, pieces):
    vmem = pl.BlockSpec(memory_space=pltpu.VMEM)
    return pl.pallas_call(
        own_kernel,
        in_specs=[vmem] * (1 + len(pieces)),
        out_specs=vmem,
        out_shape=jax.ShapeDtypeStruct((2 * ROWS + 8, 2 * ROWS), jnp.float32),
        compiler_params=pltpu.CompilerParams(vmem_limit_bytes=8 << 20),
        cost_estimate=cost(label.shape[1], 512, 256),
        name="own_tile_and_sums",
    )(label, *pieces)


def chunk_kernel(start, first, last, own_ref, label_ref, far_ref, near_ref, *refs):
    if first:
        before_ref = None
    else:
        before_ref, *refs = refs
    if last:
        *out_refs, acc = refs
    else:
        (acc,) = refs
    half = RADII * ROWS
    band, second, has_near = place()
    later = band == 1
    pieces = strips(near_ref.shape[2])

    def add(with_near):
        total = None
        for begin, end in pieces:
            own, near, far = (ref[0, :, begin:end] for ref in (own_ref, near_ref, far_ref))
            earliest = jnp.where(later, far, own)
            latest = jnp.where(later, own, far)
            label = label_ref[:, start + begin : start + end]
            rows = [annulus_rows(label)] + masked_by_annulus(earliest, label)
            if with_near:
                rows += masked_by_annulus(near, label)
            part = products(rows, jnp.concatenate([near, latest], axis=0))
            total = part if total is None else total + part
        count = total.shape[0]
        acc[:count] = total if first else total + before_ref[:count]
        if not with_near:
            acc[count:] = jnp.zeros_like(acc[count:])

    @pl.when(has_near)
    def _():
        add(True)

    @pl.when(jnp.logical_not(has_near))
    def _():
        add(False)

    if not last:
        return
    shape = (half, ROWS)
    t = lax.rem(lax.broadcasted_iota(jnp.int32, shape, 0), ROWS)
    below = lax.broadcasted_iota(jnp.int32, shape, 1) < t
    near_tile = acc[16 : 16 + half, :ROWS]
    far_tile = acc[16 : 16 + half, ROWS:]
    next_tile = acc[16 + half :, ROWS:]
    here = (jnp.where(below, near_tile, 0.0), jnp.where(below, far_tile, near_tile))
    sums = acc[:8]
    for ref, part in zip(out_refs[:2], (here, here[::-1])):
        ref[: 2 * ROWS] = packed(jnp.where(second, part[1], part[0]))
        ref[2 * ROWS :] = sums

    row = lax.broadcasted_iota(jnp.int32, (ROWS, 2 * ROWS), 0)
    lane = lax.broadcasted_iota(jnp.int32, (ROWS, 2 * ROWS), 1)
    column = lax.rem(lane, ROWS)
    tiles = packed(next_tile)
    upright = tiles[:ROWS]
    turned = tiles.T
    turned = jnp.where(lane < ROWS, pltpu.roll(turned[:ROWS], ROWS, 1), turned[ROWS:])
    low = jnp.where(column < row, upright, turned)
    high = jnp.where(column < row, turned, upright)
    diagonal = jnp.sum(jnp.where(column == row, turned, 0.0), axis=0, keepdims=True)
    beside = (lane[:8] < ROWS) & has_near
    after_sums = jnp.where(beside, pltpu.roll(sums, ROWS, 1), 0.0)
    after_sums = jnp.where(row[:8] == RADII, diagonal, after_sums)
    for ref, part in zip(out_refs[2:], ((low, high), (high, low))):
        ref[:ROWS] = jnp.where(second, part[1], part[0])
        ref[ROWS:] = after_sums


def chunk_part(piece, label, start, near, far, before, last):
    size = near.shape[2]
    acc_shape = (16 + 2 * RADII * ROWS, 2 * ROWS)
    here, after = (2 * ROWS + 8, 2 * ROWS), (ROWS + 8, 2 * ROWS)
    vmem = pl.BlockSpec(memory_space=pltpu.VMEM)
    operands = [piece, label, far, near] + ([] if before is None else [before])
    shapes = [here, here, after, after] if last else [acc_shape]
    return pl.pallas_call(
        functools.partial(chunk_kernel, start, before is None, last),
        in_specs=[vmem] * len(operands),
        out_specs=[vmem] * len(shapes),
        out_shape=[jax.ShapeDtypeStruct(shape, jnp.float32) for shape in shapes],
        scratch_shapes=[pltpu.VMEM(acc_shape, jnp.float32)] if last else [],
        compiler_params=pltpu.CompilerParams(vmem_limit_bytes=8 << 20),
        cost_estimate=cost(size, 1024, 256),
        name="chunk_tiles",
    )(*operands)


def final_kernel(factor_ref, own_ref, kept_ref, here_ref, same_ref, other_ref, out_ref):
    band, second, _ = place()
    first = jnp.logical_not(second)
    here = jnp.where(band == 0, kept_ref[...], here_ref[...])
    after = same_ref[...] + other_ref[...]
    own = own_ref[...]
    row = lax.broadcasted_iota(jnp.int32, (ROWS, 2 * ROWS), 0)
    lane = lax.broadcasted_iota(jnp.int32, (ROWS, 2 * ROWS), 1)
    column = lax.rem(lane, ROWS)
    below, above = column < row, column > row

    body = after[:ROWS]
    upright = jnp.where(below == first, body, 0.0)
    diagonal = jnp.where(column == row, after[ROWS + RADII : ROWS + RADII + 1], 0.0)
    turned = jnp.where(first, jnp.where(above, body, 0.0), jnp.where(below, body, diagonal))
    turned = jnp.concatenate([turned, turned], axis=0).T
    turned = jnp.where(lane < ROWS, turned[:ROWS], pltpu.roll(turned[ROWS:], ROWS, 1))

    ahead, present = here[2 * ROWS :] + after[ROWS:], own[2 * ROWS :]
    left = lane[:8] < ROWS
    moved = pltpu.roll(ahead, ROWS, 1)
    same = jnp.where(first, present, jnp.where(left, ahead, moved))
    beyond = jnp.where(first == left, ahead, moved)
    factor = factor_ref[...]
    for a, added in enumerate((upright, turned)):
        rows = slice(a * ROWS, (a + 1) * ROWS)
        tile = here[rows] + added + jnp.where(first, own[rows], 0.0)
        near_sum, far_sum = (
            jnp.where(left[:1], sums[a : a + 1], sums[2 + a : 3 + a]) for sums in (same, beyond)
        )
        far = jnp.where(below, far_sum, near_sum)
        tile = jnp.where(factor[rows] > 0.0, tile * factor[rows] / far, 0.0)
        swapped = pltpu.roll(tile, ROWS, 1)
        for group, twice in enumerate((jnp.where(lane < ROWS, tile, swapped), jnp.where(lane < ROWS, swapped, tile))):
            blocks = [pltpu.roll(twice[t : t + 8], 2 * ROWS - t, 1) if t else twice[:8] for t in range(0, ROWS, 8)]
            twice = jnp.concatenate(blocks, axis=0)
            for bit in range(3):
                moved = pltpu.roll(twice, 2 * ROWS - (1 << bit), 1)
                twice = jnp.where((row >> bit) & 1 == 1, moved, twice)
            out_ref[0, 2 * group + a] = twice[:, :ROWS]


def final_part(factor, own, kept, messages):
    vmem = pl.BlockSpec(memory_space=pltpu.VMEM)
    return pl.pallas_call(
        final_kernel,
        in_specs=[vmem] * (3 + len(messages)),
        out_specs=vmem,
        out_shape=jax.ShapeDtypeStruct((1, RADII, ROWS, ROWS), jnp.float32),
        compiler_params=pltpu.CompilerParams(vmem_limit_bytes=8 << 20),
        name="normalise_and_skew",
    )(factor, own, kept, *messages)


def factors(own, lag_width):
    tm, pix = lax.axis_index("tm"), lax.axis_index("pix")
    devices = lax.axis_size("tm")
    t = lax.broadcasted_iota(jnp.int32, (RADII, ROWS, ROWS), 1)
    s = lax.broadcasted_iota(jnp.int32, (RADII, ROWS, ROWS), 2)
    lag = jnp.where(s >= t, s - t, s - t + ROWS) + pix * ROWS
    valid = (lag < lag_width[0][:, None, None]) & (tm * ROWS + t + lag < devices * ROWS)
    annulus_size = PIX // RADII
    result = jnp.where(valid, annulus_size / own[:, :, None], 0.0)
    return packed(result.reshape(RADII * ROWS, ROWS))


def shards(frames, annulus_label, lag_width):
    devices = lax.axis_size("tm")
    pixels = frames.shape[2]
    pb, pix = lax.axis_index("pb"), lax.axis_index("pix")

    def far_pairs():
        for i in range(devices):
            for band, target in ((0, i - 2), (1, i + 2)):
                if 0 <= target < devices:
                    yield 2 * i + band, 2 * target + band

    def near_pairs():
        for i in range(devices):
            band, target = (0, i - 1) if i % 2 else (1, i + 1)
            if target < devices:
                yield 2 * i + band, 2 * target + band

    tm_pb = ("tm", "pb")

    def sent(piece):
        near = lax.ppermute(piece, tm_pb, list(near_pairs()))
        far = lax.ppermute(piece, tm_pb, list(far_pairs()))
        return near, far

    unit = pixels // UNITS
    starts = [sum(SIZES[:index]) * unit for index in range(len(SIZES))]
    pieces = [
        lax.slice_in_dim(frames, start, start + count * unit, axis=2) for start, count in zip(starts, SIZES)
    ]
    own = own_part(annulus_label, pieces)
    own = own + lax.ppermute(own, "pix", [(0, 1), (1, 0)])
    factor = factors(own[2 * ROWS : 2 * ROWS + RADII, :ROWS], lag_width)

    received, states, sendable = {}, [], list(pieces)

    def send(index):
        piece = pieces[index]
        if GATES[index]:
            kind, after = GATES[index]
            gate = {"done": received.get(after), "own": own, "state": states[after] if kind == "state" else None}
            piece, _ = lax.optimization_barrier((piece, gate[kind]))
        received[index] = sent(piece)

    for index in range(len(SIZES)):
        for other in range(len(SIZES)):
            gate = GATES[other]
            if other not in received and (gate is None or gate[1] < index):
                send(other)
        near, far = received[index]
        last = index == len(SIZES) - 1
        before = states[-1] if states else None
        result = chunk_part(pieces[index], annulus_label, starts[index], near, far, before, last)
        states.append(result if last else result[0])
    state = states[-1]
    here_same, here_other, after_same, after_other = state

    def swapped(message, flip):
        pairs = [
            (i * 2 + x, (i ^ 1) * 2 + (x ^ flip)) for i in range(devices) for x in range(2) if i ^ 1 < devices
        ]
        return lax.ppermute(message, ("tm", "pix"), pairs)

    beside = lax.ppermute(here_other, "pix", [(0, 1), (1, 0)])
    after = [swapped(after_same, 0), swapped(after_other, 1)]
    here = here_same + beside
    handed = lax.ppermute(here, tm_pb, [(2 * i + 1, 2 * i - 3) for i in range(2, devices)])
    return final_part(factor, own, here, [handed, *after])


def solution(mesh):
    return jax.shard_map(
        shards,
        mesh=mesh,
        in_specs=(P("pb", "tm", "pix"), P("pb", "pix"), P("pb", None)),
        out_specs=P("pb", None, "tm", "pix"),
        check_vma=False,
    )
```

```python
import functools

import jax
import jax.numpy as jnp
from jax import lax
from jax.experimental import pallas as pl
from jax.experimental.pallas import tpu as pltpu
from jax.sharding import PartitionSpec as P

DELAYS_STORED = 128
PIX = 65536
RADII = 4
ROWS = 64
UNITS = 16
SIZES = (7, 5, 3, 1)
STRIP = 2048
NT = (((1,), (1,)), ((), ()))


def place():
    band = lax.axis_index("pb")
    return band, lax.axis_index("pix") == 1, lax.rem(lax.axis_index("tm"), 2) == band


def packed(tile):
    half = tile.shape[0] // 2
    return jnp.concatenate([tile[:half], tile[half:]], axis=1)


def masked_by_annulus(block, label):
    return [block * (label == a).astype(block.dtype) for a in range(RADII)]


def annulus_rows(label):
    ids = lax.broadcasted_iota(jnp.int32, (16, label.shape[1]), 0)
    return (label == ids).astype(jnp.float32).astype(jnp.bfloat16)


def products(rows, columns):
    return lax.dot_general(
        jnp.concatenate(rows, axis=0), columns, NT, preferred_element_type=jnp.float32
    )


def strips(size):
    return [(begin, min(begin + STRIP, size)) for begin in range(0, size, STRIP)]


def own_kernel(label_ref, *refs):
    *piece_refs, out_ref = refs
    half = RADII * ROWS
    total, offset = None, 0
    for piece_ref in piece_refs:
        size = piece_ref.shape[2]
        for begin, end in strips(size):
            block = piece_ref[0, :, begin:end]
            label = label_ref[:, offset + begin : offset + end]
            part = products(masked_by_annulus(block, label) + [annulus_rows(label)], block)
            total = part if total is None else total + part
        offset += size
    tile, sums = total[:half], total[half : half + 8]
    t = lax.rem(lax.broadcasted_iota(jnp.int32, tile.shape, 0), ROWS)
    below = lax.broadcasted_iota(jnp.int32, tile.shape, 1) < t
    out_ref[: 2 * ROWS] = packed(jnp.where(below, 0.0, tile))
    out_ref[2 * ROWS :] = jnp.concatenate([sums, sums], axis=1)


def cost(pixels, rows, columns):
    return pl.CostEstimate(
        flops=2 * rows * columns * pixels, bytes_accessed=2 * columns * pixels, transcendentals=0
    )


def own_part(label, pieces):
    vmem = pl.BlockSpec(memory_space=pltpu.VMEM)
    return pl.pallas_call(
        own_kernel,
        in_specs=[vmem] * (1 + len(pieces)),
        out_specs=vmem,
        out_shape=jax.ShapeDtypeStruct((2 * ROWS + 8, 2 * ROWS), jnp.float32),
        compiler_params=pltpu.CompilerParams(vmem_limit_bytes=8 << 20),
        cost_estimate=cost(label.shape[1], 512, 256),
        name="own_tile_and_sums",
    )(label, *pieces)


def chunk_kernel(start, first, last, own_ref, label_ref, *refs):
    if first:
        far_alone_ref, near_ref, far_ref, *refs = refs
    else:
        far_ref, near_ref, *refs = refs
        far_alone_ref = far_ref
    if first:
        before_ref = None
    else:
        before_ref, *refs = refs
    if not last:
        _, *refs = refs
    if last:
        *out_refs, acc = refs
    else:
        (acc,) = refs
    half = RADII * ROWS
    band, second, has_near = place()
    later = band == 1
    pieces = strips(near_ref.shape[2])

    def add(with_near):
        total = None
        sources = (own_ref, near_ref, far_ref if with_near else far_alone_ref)
        for begin, end in pieces:
            own, near, far = (ref[0, :, begin:end] for ref in sources)
            earliest = jnp.where(later, far, own)
            latest = jnp.where(later, own, far)
            label = label_ref[:, start + begin : start + end]
            rows = [annulus_rows(label)] + masked_by_annulus(earliest, label)
            if with_near:
                rows += masked_by_annulus(near, label)
            part = products(rows, jnp.concatenate([near, latest], axis=0))
            total = part if total is None else total + part
        count = total.shape[0]
        acc[:count] = total if first else total + before_ref[:count]
        if not with_near:
            acc[count:] = jnp.zeros_like(acc[count:])

    @pl.when(has_near)
    def _():
        add(True)

    @pl.when(jnp.logical_not(has_near))
    def _():
        add(False)

    if not last:
        return
    shape = (half, ROWS)
    t = lax.rem(lax.broadcasted_iota(jnp.int32, shape, 0), ROWS)
    below = lax.broadcasted_iota(jnp.int32, shape, 1) < t
    near_tile = acc[16 : 16 + half, :ROWS]
    far_tile = acc[16 : 16 + half, ROWS:]
    next_tile = acc[16 + half :, ROWS:]
    here = (jnp.where(below, near_tile, 0.0), jnp.where(below, far_tile, near_tile))
    sums = acc[:8]
    for ref, part in zip(out_refs[:2], (here, here[::-1])):
        ref[: 2 * ROWS] = packed(jnp.where(second, part[1], part[0]))
        ref[2 * ROWS :] = sums

    row = lax.broadcasted_iota(jnp.int32, (ROWS, 2 * ROWS), 0)
    lane = lax.broadcasted_iota(jnp.int32, (ROWS, 2 * ROWS), 1)
    column = lax.rem(lane, ROWS)
    tiles = packed(next_tile)
    upright = tiles[:ROWS]
    turned = tiles.T
    turned = jnp.where(lane < ROWS, pltpu.roll(turned[:ROWS], ROWS, 1), turned[ROWS:])
    low = jnp.where(column < row, upright, turned)
    high = jnp.where(column < row, turned, upright)
    diagonal = jnp.sum(jnp.where(column == row, turned, 0.0), axis=0, keepdims=True)
    beside = (lane[:8] < ROWS) & has_near
    after_sums = jnp.where(beside, pltpu.roll(sums, ROWS, 1), 0.0)
    after_sums = jnp.where(row[:8] == RADII, diagonal, after_sums)
    for ref, part in zip(out_refs[2:], ((low, high), (high, low))):
        ref[:ROWS] = jnp.where(second, part[1], part[0])
        ref[ROWS:] = after_sums


def chunk_part(piece, label, start, far, near, before, awaited, last):
    size = piece.shape[2]
    acc_shape = (16 + 2 * RADII * ROWS, 2 * ROWS)
    here, after = (2 * ROWS + 8, 2 * ROWS), (ROWS + 8, 2 * ROWS)
    vmem = pl.BlockSpec(memory_space=pltpu.VMEM)
    operands = [piece, label, far[0], near, *far[1:]] + ([] if before is None else [before])
    if not last:
        operands.append(awaited)
    shapes = [here, here, after, after] if last else [acc_shape]
    return pl.pallas_call(
        functools.partial(chunk_kernel, start, before is None, last),
        in_specs=[vmem] * len(operands),
        out_specs=[vmem] * len(shapes),
        out_shape=[jax.ShapeDtypeStruct(shape, jnp.float32) for shape in shapes],
        scratch_shapes=[pltpu.VMEM(acc_shape, jnp.float32)] if last else [],
        compiler_params=pltpu.CompilerParams(vmem_limit_bytes=8 << 20),
        cost_estimate=cost(size, 1024, 256),
        name="chunk_tiles",
    )(*operands)


def final_kernel(factor_ref, own_ref, kept_ref, here_ref, same_ref, other_ref, out_ref):
    band, second, _ = place()
    first = jnp.logical_not(second)
    here = jnp.where(band == 0, kept_ref[...], here_ref[...])
    after = same_ref[...] + other_ref[...]
    own = own_ref[...]
    row = lax.broadcasted_iota(jnp.int32, (ROWS, 2 * ROWS), 0)
    lane = lax.broadcasted_iota(jnp.int32, (ROWS, 2 * ROWS), 1)
    column = lax.rem(lane, ROWS)
    below, above = column < row, column > row

    body = after[:ROWS]
    upright = jnp.where(below == first, body, 0.0)
    diagonal = jnp.where(column == row, after[ROWS + RADII : ROWS + RADII + 1], 0.0)
    turned = jnp.where(first, jnp.where(above, body, 0.0), jnp.where(below, body, diagonal))
    turned = jnp.concatenate([turned, turned], axis=0).T
    turned = jnp.where(lane < ROWS, turned[:ROWS], pltpu.roll(turned[ROWS:], ROWS, 1))

    ahead, present = here[2 * ROWS :] + after[ROWS:], own[2 * ROWS :]
    left = lane[:8] < ROWS
    moved = pltpu.roll(ahead, ROWS, 1)
    same = jnp.where(first, present, jnp.where(left, ahead, moved))
    beyond = jnp.where(first == left, ahead, moved)
    factor = factor_ref[...]
    for a, added in enumerate((upright, turned)):
        rows = slice(a * ROWS, (a + 1) * ROWS)
        tile = here[rows] + added + jnp.where(first, own[rows], 0.0)
        near_sum, far_sum = (
            jnp.where(left[:1], sums[a : a + 1], sums[2 + a : 3 + a]) for sums in (same, beyond)
        )
        far = jnp.where(below, far_sum, near_sum)
        tile = jnp.where(factor[rows] > 0.0, tile * factor[rows] / far, 0.0)
        swapped = pltpu.roll(tile, ROWS, 1)
        for group, twice in enumerate((jnp.where(lane < ROWS, tile, swapped), jnp.where(lane < ROWS, swapped, tile))):
            blocks = [pltpu.roll(twice[t : t + 8], 2 * ROWS - t, 1) if t else twice[:8] for t in range(0, ROWS, 8)]
            twice = jnp.concatenate(blocks, axis=0)
            for bit in range(3):
                moved = pltpu.roll(twice, 2 * ROWS - (1 << bit), 1)
                twice = jnp.where((row >> bit) & 1 == 1, moved, twice)
            out_ref[0, 2 * group + a] = twice[:, :ROWS]


def final_part(factor, own, kept, messages):
    vmem = pl.BlockSpec(memory_space=pltpu.VMEM)
    return pl.pallas_call(
        final_kernel,
        in_specs=[vmem] * (3 + len(messages)),
        out_specs=vmem,
        out_shape=jax.ShapeDtypeStruct((1, RADII, ROWS, ROWS), jnp.float32),
        compiler_params=pltpu.CompilerParams(vmem_limit_bytes=8 << 20),
        name="normalise_and_skew",
    )(factor, own, kept, *messages)


def factors(own, lag_width):
    tm, pix = lax.axis_index("tm"), lax.axis_index("pix")
    devices = lax.axis_size("tm")
    t = lax.broadcasted_iota(jnp.int32, (RADII, ROWS, ROWS), 1)
    s = lax.broadcasted_iota(jnp.int32, (RADII, ROWS, ROWS), 2)
    lag = jnp.where(s >= t, s - t, s - t + ROWS) + pix * ROWS
    valid = (lag < lag_width[0][:, None, None]) & (tm * ROWS + t + lag < devices * ROWS)
    annulus_size = PIX // RADII
    result = jnp.where(valid, annulus_size / own[:, :, None], 0.0)
    return packed(result.reshape(RADII * ROWS, ROWS))


def shards(frames, annulus_label, lag_width):
    devices = lax.axis_size("tm")
    pixels = frames.shape[2]
    pb, pix = lax.axis_index("pb"), lax.axis_index("pix")

    def far_pairs(parities):
        for i in range(devices):
            for band, target in ((0, i - 2), (1, i + 2)):
                if 0 <= target < devices and (i % 2 == band) in parities:
                    yield 2 * i + band, 2 * target + band

    def near_pairs():
        for i in range(devices):
            band, target = (0, i - 1) if i % 2 else (1, i + 1)
            if target < devices:
                yield 2 * i + band, 2 * target + band

    tm_pb = ("tm", "pb")

    def sent(piece, first):
        def far(*parities):
            return lax.ppermute(piece, tm_pb, list(far_pairs(parities)))

        if not first:
            alone = far(False, True)
            return [alone], lax.ppermute(piece, tm_pb, list(near_pairs()))
        alone = far(False)
        near = lax.ppermute(piece, tm_pb, list(near_pairs()))
        return [alone, far(True)], near

    unit = pixels // UNITS
    starts = [sum(SIZES[:index]) * unit for index in range(len(SIZES))]
    pieces = [
        lax.slice_in_dim(frames, start, start + count * unit, axis=2) for start, count in zip(starts, SIZES)
    ]
    own = own_part(annulus_label, pieces)
    received = [sent(piece, index == 0) for index, piece in enumerate(pieces)]
    own, _ = lax.optimization_barrier((own, received[0]))
    own = own + lax.ppermute(own, "pix", [(0, 1), (1, 0)])
    factor = factors(own[2 * ROWS : 2 * ROWS + RADII, :ROWS], lag_width)

    states = []
    for index, (piece, (far, near)) in enumerate(zip(pieces, received)):
        last = index == len(SIZES) - 1
        before = states[-1] if states else None
        awaited = own
        if index == 0:
            corner = lax.optimization_barrier(far[0][:, :8, :128])
            awaited = corner + near[:, :8, :128]
        result = chunk_part(piece, annulus_label, starts[index], far, near, before, awaited, last)
        states.append(result if last else result[0])
    state = states[-1]
    here_same, here_other, after_same, after_other = state

    def swapped(message, flip):
        pairs = [
            (i * 2 + x, (i ^ 1) * 2 + (x ^ flip)) for i in range(devices) for x in range(2) if i ^ 1 < devices
        ]
        return lax.ppermute(message, ("tm", "pix"), pairs)

    beside = lax.ppermute(here_other, "pix", [(0, 1), (1, 0)])
    after = [swapped(after_same, 0), swapped(after_other, 1)]
    here = here_same + beside
    handed = lax.ppermute(here, tm_pb, [(2 * i + 1, 2 * i - 3) for i in range(2, devices)])
    return final_part(factor, own, here, [handed, *after])


def solution(mesh):
    return jax.shard_map(
        shards,
        mesh=mesh,
        in_specs=(P("pb", "tm", "pix"), P("pb", "pix"), P("pb", None)),
        out_specs=P("pb", None, "tm", "pix"),
        check_vma=False,
    )
```

```python
import functools

import jax
import jax.numpy as jnp
from jax import lax
from jax.experimental import pallas as pl
from jax.experimental.pallas import tpu as pltpu
from jax.sharding import PartitionSpec as P

DELAYS_STORED = 128
PIX = 65536
RADII = 4
ROWS = 64
UNITS = 16
SIZES = (4, 8, 3, 1)
STRIP = 2048
NT = (((1,), (1,)), ((), ()))


def place():
    band = lax.axis_index("pb")
    return band, lax.axis_index("pix") == 1, lax.rem(lax.axis_index("tm"), 2) == band


def packed(tile):
    half = tile.shape[0] // 2
    return jnp.concatenate([tile[:half], tile[half:]], axis=1)


def masked_by_annulus(block, label):
    return [block * (label == a).astype(block.dtype) for a in range(RADII)]


def annulus_rows(label):
    ids = lax.broadcasted_iota(jnp.int32, (16, label.shape[1]), 0)
    return (label == ids).astype(jnp.float32).astype(jnp.bfloat16)


def products(rows, columns):
    return lax.dot_general(
        jnp.concatenate(rows, axis=0), columns, NT, preferred_element_type=jnp.float32
    )


def strips(size):
    return [(begin, min(begin + STRIP, size)) for begin in range(0, size, STRIP)]


def later_kernel(starts, frames_ref, *refs):
    count = len(starts)
    piece_refs, stage_refs, (in_semaphore, out_semaphore) = refs[:count], refs[count : 2 * count], refs[2 * count :]
    reads, writes = [], []
    for index, (start, piece_ref, stage_ref) in enumerate(zip(starts, piece_refs, stage_refs)):
        source = frames_ref.at[:, :, start : start + piece_ref.shape[2]]
        reads.append(pltpu.make_async_copy(source, stage_ref, in_semaphore.at[index]))
        writes.append(pltpu.make_async_copy(stage_ref, piece_ref, out_semaphore.at[index]))
    for read in reads:
        read.start()
    for read, write in zip(reads, writes):
        read.wait()
        write.start()
    for write in writes:
        write.wait()


def later_pieces(frames, starts):
    unit = frames.shape[2] // UNITS
    shapes = [(1, ROWS, count * unit) for count in SIZES[1:]]
    semaphores = pltpu.SemaphoreType.DMA((len(shapes),))
    return pl.pallas_call(
        functools.partial(later_kernel, starts),
        in_specs=[pl.BlockSpec(memory_space=pl.ANY)],
        out_specs=[pl.BlockSpec(memory_space=pl.ANY)] * len(shapes),
        out_shape=[jax.ShapeDtypeStruct(shape, frames.dtype) for shape in shapes],
        scratch_shapes=[pltpu.VMEM(shape, frames.dtype) for shape in shapes] + [semaphores] * 2,
        compiler_params=pltpu.CompilerParams(vmem_limit_bytes=60 << 20),
        name="later_pieces",
    )(frames)


def own_kernel(label_ref, *refs):
    *piece_refs, out_ref, copy_ref = refs
    copy_ref[...] = piece_refs[2][...]
    half = RADII * ROWS
    total, offset = None, 0
    for piece_ref in piece_refs:
        size = piece_ref.shape[2]
        for begin, end in strips(size):
            block = piece_ref[0, :, begin:end]
            label = label_ref[:, offset + begin : offset + end]
            part = products(masked_by_annulus(block, label) + [annulus_rows(label)], block)
            total = part if total is None else total + part
        offset += size
    tile, sums = total[:half], total[half : half + 8]
    t = lax.rem(lax.broadcasted_iota(jnp.int32, tile.shape, 0), ROWS)
    below = lax.broadcasted_iota(jnp.int32, tile.shape, 1) < t
    out_ref[: 2 * ROWS] = packed(jnp.where(below, 0.0, tile))
    out_ref[2 * ROWS :] = jnp.concatenate([sums, sums], axis=1)


def cost(pixels, rows, columns):
    return pl.CostEstimate(
        flops=2 * rows * columns * pixels, bytes_accessed=2 * columns * pixels, transcendentals=0
    )


def own_part(label, pieces):
    vmem = pl.BlockSpec(memory_space=pltpu.VMEM)
    return pl.pallas_call(
        own_kernel,
        in_specs=[vmem] * (1 + len(pieces)),
        out_specs=[vmem] * 2,
        out_shape=[
            jax.ShapeDtypeStruct((2 * ROWS + 8, 2 * ROWS), jnp.float32),
            jax.ShapeDtypeStruct(pieces[2].shape, pieces[2].dtype),
        ],
        compiler_params=pltpu.CompilerParams(vmem_limit_bytes=8 << 20),
        cost_estimate=cost(label.shape[1], 512, 256),
        name="own_tile_and_sums",
    )(label, *pieces)


def chunk_kernel(start, first, last, own_ref, label_ref, *refs):
    if first:
        far_alone_ref, near_ref, far_ref, *refs = refs
    else:
        far_ref, near_ref, *refs = refs
        far_alone_ref = far_ref
    if first:
        before_ref = None
    else:
        before_ref, *refs = refs
    if not last:
        _, *refs = refs
    if last:
        *out_refs, acc = refs
    else:
        (acc,) = refs
    half = RADII * ROWS
    band, second, has_near = place()
    later = band == 1
    pieces = strips(near_ref.shape[2])

    def add(with_near):
        total = None
        sources = (own_ref, near_ref, far_ref if with_near else far_alone_ref)
        for begin, end in pieces:
            own, near, far = (ref[0, :, begin:end] for ref in sources)
            earliest = jnp.where(later, far, own)
            latest = jnp.where(later, own, far)
            label = label_ref[:, start + begin : start + end]
            rows = [annulus_rows(label)] + masked_by_annulus(earliest, label)
            if with_near:
                rows += masked_by_annulus(near, label)
            part = products(rows, jnp.concatenate([near, latest], axis=0))
            total = part if total is None else total + part
        count = total.shape[0]
        acc[:count] = total if first else total + before_ref[:count]
        if not with_near:
            acc[count:] = jnp.zeros_like(acc[count:])

    @pl.when(has_near)
    def _():
        add(True)

    @pl.when(jnp.logical_not(has_near))
    def _():
        add(False)

    if not last:
        return
    shape = (half, ROWS)
    t = lax.rem(lax.broadcasted_iota(jnp.int32, shape, 0), ROWS)
    below = lax.broadcasted_iota(jnp.int32, shape, 1) < t
    near_tile = acc[16 : 16 + half, :ROWS]
    far_tile = acc[16 : 16 + half, ROWS:]
    next_tile = acc[16 + half :, ROWS:]
    here = (jnp.where(below, near_tile, 0.0), jnp.where(below, far_tile, near_tile))
    sums = acc[:8]
    for ref, part in zip(out_refs[:2], (here, here[::-1])):
        ref[: 2 * ROWS] = packed(jnp.where(second, part[1], part[0]))
        ref[2 * ROWS :] = sums

    row = lax.broadcasted_iota(jnp.int32, (ROWS, 2 * ROWS), 0)
    lane = lax.broadcasted_iota(jnp.int32, (ROWS, 2 * ROWS), 1)
    column = lax.rem(lane, ROWS)
    tiles = packed(next_tile)
    upright = tiles[:ROWS]
    turned = tiles.T
    turned = jnp.where(lane < ROWS, pltpu.roll(turned[:ROWS], ROWS, 1), turned[ROWS:])
    low = jnp.where(column < row, upright, turned)
    high = jnp.where(column < row, turned, upright)
    diagonal = jnp.sum(jnp.where(column == row, turned, 0.0), axis=0, keepdims=True)
    beside = (lane[:8] < ROWS) & has_near
    after_sums = jnp.where(beside, pltpu.roll(sums, ROWS, 1), 0.0)
    after_sums = jnp.where(row[:8] == RADII, diagonal, after_sums)
    for ref, part in zip(out_refs[2:], ((low, high), (high, low))):
        ref[:ROWS] = jnp.where(second, part[1], part[0])
        ref[ROWS:] = after_sums


def chunk_part(piece, label, start, far, near, before, awaited, last):
    size = piece.shape[2]
    acc_shape = (16 + 2 * RADII * ROWS, 2 * ROWS)
    here, after = (2 * ROWS + 8, 2 * ROWS), (ROWS + 8, 2 * ROWS)
    vmem = pl.BlockSpec(memory_space=pltpu.VMEM)
    operands = [piece, label, far[0], near, *far[1:]] + ([] if before is None else [before])
    if not last:
        operands.append(awaited)
    shapes = [here, here, after, after] if last else [acc_shape]
    return pl.pallas_call(
        functools.partial(chunk_kernel, start, before is None, last),
        in_specs=[vmem] * len(operands),
        out_specs=[vmem] * len(shapes),
        out_shape=[jax.ShapeDtypeStruct(shape, jnp.float32) for shape in shapes],
        scratch_shapes=[pltpu.VMEM(acc_shape, jnp.float32)] if last else [],
        compiler_params=pltpu.CompilerParams(vmem_limit_bytes=8 << 20),
        cost_estimate=cost(size if before is not None else 20 * size, 1024, 256),
        name="chunk_tiles",
    )(*operands)


def final_kernel(factor_ref, own_ref, kept_ref, here_ref, same_ref, other_ref, out_ref):
    band, second, _ = place()
    first = jnp.logical_not(second)
    here = jnp.where(band == 0, kept_ref[...], here_ref[...])
    after = same_ref[...] + other_ref[...]
    own = own_ref[...]
    row = lax.broadcasted_iota(jnp.int32, (ROWS, 2 * ROWS), 0)
    lane = lax.broadcasted_iota(jnp.int32, (ROWS, 2 * ROWS), 1)
    column = lax.rem(lane, ROWS)
    below, above = column < row, column > row

    body = after[:ROWS]
    upright = jnp.where(below == first, body, 0.0)
    diagonal = jnp.where(column == row, after[ROWS + RADII : ROWS + RADII + 1], 0.0)
    turned = jnp.where(first, jnp.where(above, body, 0.0), jnp.where(below, body, diagonal))
    turned = jnp.concatenate([turned, turned], axis=0).T
    turned = jnp.where(lane < ROWS, turned[:ROWS], pltpu.roll(turned[ROWS:], ROWS, 1))

    ahead, present = here[2 * ROWS :] + after[ROWS:], own[2 * ROWS :]
    left = lane[:8] < ROWS
    moved = pltpu.roll(ahead, ROWS, 1)
    same = jnp.where(first, present, jnp.where(left, ahead, moved))
    beyond = jnp.where(first == left, ahead, moved)
    factor = factor_ref[...]
    for a, added in enumerate((upright, turned)):
        rows = slice(a * ROWS, (a + 1) * ROWS)
        tile = here[rows] + added + jnp.where(first, own[rows], 0.0)
        near_sum, far_sum = (
            jnp.where(left[:1], sums[a : a + 1], sums[2 + a : 3 + a]) for sums in (same, beyond)
        )
        far = jnp.where(below, far_sum, near_sum)
        tile = jnp.where(factor[rows] > 0.0, tile * factor[rows] / far, 0.0)
        swapped = pltpu.roll(tile, ROWS, 1)
        for group, twice in enumerate((jnp.where(lane < ROWS, tile, swapped), jnp.where(lane < ROWS, swapped, tile))):
            blocks = [pltpu.roll(twice[t : t + 8], 2 * ROWS - t, 1) if t else twice[:8] for t in range(0, ROWS, 8)]
            twice = jnp.concatenate(blocks, axis=0)
            for bit in range(3):
                moved = pltpu.roll(twice, 2 * ROWS - (1 << bit), 1)
                twice = jnp.where((row >> bit) & 1 == 1, moved, twice)
            out_ref[0, 2 * group + a] = twice[:, :ROWS]


def final_part(factor, own, kept, messages):
    vmem = pl.BlockSpec(memory_space=pltpu.VMEM)
    return pl.pallas_call(
        final_kernel,
        in_specs=[vmem] * (3 + len(messages)),
        out_specs=vmem,
        out_shape=jax.ShapeDtypeStruct((1, RADII, ROWS, ROWS), jnp.float32),
        compiler_params=pltpu.CompilerParams(vmem_limit_bytes=8 << 20),
        name="normalise_and_skew",
    )(factor, own, kept, *messages)


def factors(own, lag_width):
    tm, pix = lax.axis_index("tm"), lax.axis_index("pix")
    devices = lax.axis_size("tm")
    t = lax.broadcasted_iota(jnp.int32, (RADII, ROWS, ROWS), 1)
    s = lax.broadcasted_iota(jnp.int32, (RADII, ROWS, ROWS), 2)
    lag = jnp.where(s >= t, s - t, s - t + ROWS) + pix * ROWS
    valid = (lag < lag_width[0][:, None, None]) & (tm * ROWS + t + lag < devices * ROWS)
    annulus_size = PIX // RADII
    result = jnp.where(valid, annulus_size / own[:, :, None], 0.0)
    return packed(result.reshape(RADII * ROWS, ROWS))


def shards(frames, annulus_label, lag_width):
    devices = lax.axis_size("tm")
    pixels = frames.shape[2]
    pb, pix = lax.axis_index("pb"), lax.axis_index("pix")

    def far_pairs(parities):
        for i in range(devices):
            for band, target in ((0, i - 2), (1, i + 2)):
                if 0 <= target < devices and (i % 2 == band) in parities:
                    yield 2 * i + band, 2 * target + band

    def near_pairs():
        for i in range(devices):
            band, target = (0, i - 1) if i % 2 else (1, i + 1)
            if target < devices:
                yield 2 * i + band, 2 * target + band

    tm_pb = ("tm", "pb")

    def sent(piece, first):
        def far(*parities):
            return lax.ppermute(piece, tm_pb, list(far_pairs(parities)))

        if not first:
            alone = far(False, True)
            return [alone], lax.ppermute(piece, tm_pb, list(near_pairs()))
        alone = far(False)
        near = lax.ppermute(piece, tm_pb, list(near_pairs()))
        return [alone, far(True)], near

    unit = pixels // UNITS
    starts = [sum(SIZES[:index]) * unit for index in range(len(SIZES))]
    pieces = [lax.slice_in_dim(frames, 0, SIZES[0] * unit, axis=2), *later_pieces(frames, starts[1:])]
    own, third = own_part(annulus_label, pieces)
    received = [sent(piece, index == 0) for index, piece in enumerate(pieces)]
    own, _ = lax.optimization_barrier((own, received[0]))
    own = own + lax.ppermute(own, "pix", [(0, 1), (1, 0)])
    factor = factors(own[2 * ROWS : 2 * ROWS + RADII, :ROWS], lag_width)

    pieces[2] = third
    states = []
    for index, (piece, (far, near)) in enumerate(zip(pieces, received)):
        last = index == len(SIZES) - 1
        before = states[-1] if states else None
        awaited = own
        if index == 0:
            corner = lax.optimization_barrier(far[0][:, :8, :128])
            awaited = corner + near[:, :8, :128]
        result = chunk_part(piece, annulus_label, starts[index], far, near, before, awaited, last)
        states.append(result if last else result[0])
    state = states[-1]
    here_same, here_other, after_same, after_other = state

    def swapped(message, flip):
        pairs = [
            (i * 2 + x, (i ^ 1) * 2 + (x ^ flip)) for i in range(devices) for x in range(2) if i ^ 1 < devices
        ]
        return lax.ppermute(message, ("tm", "pix"), pairs)

    beside = lax.ppermute(here_other, "pix", [(0, 1), (1, 0)])
    after = [swapped(after_same, 0), swapped(after_other, 1)]
    here = here_same + beside
    handed = lax.ppermute(here, tm_pb, [(2 * i + 1, 2 * i - 3) for i in range(2, devices)])
    return final_part(factor, own, here, [handed, *after])


def solution(mesh):
    return jax.shard_map(
        shards,
        mesh=mesh,
        in_specs=(P("pb", "tm", "pix"), P("pb", "pix"), P("pb", None)),
        out_specs=P("pb", None, "tm", "pix"),
        check_vma=False,
    )
```

```python
import functools

import jax
import jax.numpy as jnp
from jax import lax
from jax.experimental import pallas as pl
from jax.experimental.pallas import tpu as pltpu
from jax.sharding import PartitionSpec as P

DELAYS_STORED = 128
PIX = 65536
RADII = 4
ROWS = 64
UNITS = 16
SIZES = (4, 8, 3, 1)
STRIP = 2048
NT = (((1,), (1,)), ((), ()))


def place():
    band = lax.axis_index("pb")
    return band, lax.axis_index("pix") == 1, lax.rem(lax.axis_index("tm"), 2) == band


def packed(tile):
    half = tile.shape[0] // 2
    return jnp.concatenate([tile[:half], tile[half:]], axis=1)


def masked_by_annulus(block, label):
    return [block * (label == a).astype(block.dtype) for a in range(RADII)]


def annulus_rows(label):
    ids = lax.broadcasted_iota(jnp.int32, (16, label.shape[1]), 0)
    return (label == ids).astype(jnp.float32).astype(jnp.bfloat16)


def products(rows, columns):
    return lax.dot_general(
        jnp.concatenate(rows, axis=0), columns, NT, preferred_element_type=jnp.float32
    )


def strips(size):
    return [(begin, min(begin + STRIP, size)) for begin in range(0, size, STRIP)]


def later_kernel(starts, frames_ref, *refs):
    count = len(starts)
    piece_refs, stage_refs, (in_semaphore, out_semaphore) = refs[:count], refs[count : 2 * count], refs[2 * count :]
    reads, writes = [], []
    for index, (start, piece_ref, stage_ref) in enumerate(zip(starts, piece_refs, stage_refs)):
        source = frames_ref.at[:, :, start : start + piece_ref.shape[2]]
        reads.append(pltpu.make_async_copy(source, stage_ref, in_semaphore.at[index]))
        writes.append(pltpu.make_async_copy(stage_ref, piece_ref, out_semaphore.at[index]))
    for read in reads:
        read.start()
    for read, write in zip(reads, writes):
        read.wait()
        write.start()
    for write in writes:
        write.wait()


def later_pieces(frames, starts):
    unit = frames.shape[2] // UNITS
    shapes = [(1, ROWS, count * unit) for count in SIZES[1:]]
    semaphores = pltpu.SemaphoreType.DMA((len(shapes),))
    return pl.pallas_call(
        functools.partial(later_kernel, starts),
        in_specs=[pl.BlockSpec(memory_space=pl.ANY)],
        out_specs=[pl.BlockSpec(memory_space=pl.ANY)] * len(shapes),
        out_shape=[jax.ShapeDtypeStruct(shape, frames.dtype) for shape in shapes],
        scratch_shapes=[pltpu.VMEM(shape, frames.dtype) for shape in shapes] + [semaphores] * 2,
        compiler_params=pltpu.CompilerParams(vmem_limit_bytes=60 << 20),
        name="later_pieces",
    )(frames)


def own_kernel(label_ref, *refs):
    *piece_refs, out_ref, copy_ref = refs
    copy_ref[...] = piece_refs[2][...]
    half = RADII * ROWS
    total, offset = None, 0
    for piece_ref in piece_refs:
        size = piece_ref.shape[2]
        for begin, end in strips(size):
            block = piece_ref[0, :, begin:end]
            label = label_ref[:, offset + begin : offset + end]
            part = products(masked_by_annulus(block, label) + [annulus_rows(label)], block)
            total = part if total is None else total + part
        offset += size
    tile, sums = total[:half], total[half : half + 8]
    t = lax.rem(lax.broadcasted_iota(jnp.int32, tile.shape, 0), ROWS)
    below = lax.broadcasted_iota(jnp.int32, tile.shape, 1) < t
    out_ref[: 2 * ROWS] = packed(jnp.where(below, 0.0, tile))
    out_ref[2 * ROWS :] = jnp.concatenate([sums, sums], axis=1)


def cost(pixels, rows, columns):
    return pl.CostEstimate(
        flops=2 * rows * columns * pixels, bytes_accessed=2 * columns * pixels, transcendentals=0
    )


def own_part(label, pieces):
    vmem = pl.BlockSpec(memory_space=pltpu.VMEM)
    return pl.pallas_call(
        own_kernel,
        in_specs=[vmem] * (1 + len(pieces)),
        out_specs=[vmem] * 2,
        out_shape=[
            jax.ShapeDtypeStruct((2 * ROWS + 8, 2 * ROWS), jnp.float32),
            jax.ShapeDtypeStruct(pieces[2].shape, pieces[2].dtype),
        ],
        compiler_params=pltpu.CompilerParams(vmem_limit_bytes=8 << 20),
        cost_estimate=cost(label.shape[1], 512, 256),
        name="own_tile_and_sums",
    )(label, *pieces)


def chunk_kernel(start, first, last, own_ref, label_ref, far_ref, near_ref, *refs):
    if not first:
        before_ref, *refs = refs
    if last:
        *out_refs, acc = refs
    else:
        _, acc = refs
    half = RADII * ROWS
    band, second, has_near = place()
    later = band == 1
    pieces = strips(near_ref.shape[2])

    def add(with_near):
        total = None
        for begin, end in pieces:
            own, near, far = (ref[0, :, begin:end] for ref in (own_ref, near_ref, far_ref))
            earliest = jnp.where(later, far, own)
            latest = jnp.where(later, own, far)
            label = label_ref[:, start + begin : start + end]
            rows = [annulus_rows(label)] + masked_by_annulus(earliest, label)
            if with_near:
                rows += masked_by_annulus(near, label)
            else:
                near = jnp.zeros_like(near)
            part = products(rows, jnp.concatenate([near, latest], axis=0))
            total = part if total is None else total + part
        count = total.shape[0]
        acc[:count] = total if first else total + before_ref[:count]
        if not with_near:
            acc[count:] = jnp.zeros_like(acc[count:])

    @pl.when(has_near)
    def _():
        add(True)

    @pl.when(jnp.logical_not(has_near))
    def _():
        add(False)

    if not last:
        return
    shape = (half, ROWS)
    t = lax.rem(lax.broadcasted_iota(jnp.int32, shape, 0), ROWS)
    below = lax.broadcasted_iota(jnp.int32, shape, 1) < t
    near_tile = acc[16 : 16 + half, :ROWS]
    far_tile = acc[16 : 16 + half, ROWS:]
    next_tile = acc[16 + half :, ROWS:]
    here = (jnp.where(below, near_tile, 0.0), jnp.where(below, far_tile, near_tile))
    sums = acc[:8]
    for ref, part in zip(out_refs[:2], (here, here[::-1])):
        ref[: 2 * ROWS] = packed(jnp.where(second, part[1], part[0]))
        ref[2 * ROWS :] = sums

    row = lax.broadcasted_iota(jnp.int32, (ROWS, 2 * ROWS), 0)
    lane = lax.broadcasted_iota(jnp.int32, (ROWS, 2 * ROWS), 1)
    column = lax.rem(lane, ROWS)
    tiles = packed(next_tile)
    upright = tiles[:ROWS]
    turned = tiles.T
    turned = jnp.where(lane < ROWS, pltpu.roll(turned[:ROWS], ROWS, 1), turned[ROWS:])
    low = jnp.where(column < row, upright, turned)
    high = jnp.where(column < row, turned, upright)
    diagonal = jnp.sum(jnp.where(column == row, turned, 0.0), axis=0, keepdims=True)
    beside = (lane[:8] < ROWS) & has_near
    after_sums = jnp.where(beside, pltpu.roll(sums, ROWS, 1), 0.0)
    after_sums = jnp.where(row[:8] == RADII, diagonal, after_sums)
    for ref, part in zip(out_refs[2:], ((low, high), (high, low))):
        ref[:ROWS] = jnp.where(second, part[1], part[0])
        ref[ROWS:] = after_sums


def chunk_part(piece, label, start, far, near, before, awaited, last):
    size = piece.shape[2]
    acc_shape = (16 + 2 * RADII * ROWS, 2 * ROWS)
    here, after = (2 * ROWS + 8, 2 * ROWS), (ROWS + 8, 2 * ROWS)
    vmem = pl.BlockSpec(memory_space=pltpu.VMEM)
    operands = [piece, label, far, near] + ([] if before is None else [before])
    if not last:
        operands.append(awaited)
    shapes = [here, here, after, after] if last else [acc_shape]
    return pl.pallas_call(
        functools.partial(chunk_kernel, start, before is None, last),
        in_specs=[vmem] * len(operands),
        out_specs=[vmem] * len(shapes),
        out_shape=[jax.ShapeDtypeStruct(shape, jnp.float32) for shape in shapes],
        scratch_shapes=[pltpu.VMEM(acc_shape, jnp.float32)] if last else [],
        compiler_params=pltpu.CompilerParams(vmem_limit_bytes=8 << 20),
        cost_estimate=cost(size if before is not None else 20 * size, 1024, 256),
        name="chunk_tiles",
    )(*operands)


def final_kernel(factor_ref, own_ref, kept_ref, here_ref, same_ref, other_ref, out_ref):
    band, second, _ = place()
    first = jnp.logical_not(second)
    inside = lax.axis_index("tm") < lax.axis_size("tm") - 2
    here = jnp.where(band == 0, kept_ref[...], jnp.where(inside, here_ref[...], 0.0))
    after = same_ref[...] + other_ref[...]
    own = own_ref[...]
    row = lax.broadcasted_iota(jnp.int32, (ROWS, 2 * ROWS), 0)
    lane = lax.broadcasted_iota(jnp.int32, (ROWS, 2 * ROWS), 1)
    column = lax.rem(lane, ROWS)
    below, above = column < row, column > row

    body = after[:ROWS]
    upright = jnp.where(below == first, body, 0.0)
    diagonal = jnp.where(column == row, after[ROWS + RADII : ROWS + RADII + 1], 0.0)
    turned = jnp.where(first, jnp.where(above, body, 0.0), jnp.where(below, body, diagonal))
    turned = jnp.concatenate([turned, turned], axis=0).T
    turned = jnp.where(lane < ROWS, turned[:ROWS], pltpu.roll(turned[ROWS:], ROWS, 1))

    ahead, present = here[2 * ROWS :] + after[ROWS:], own[2 * ROWS :]
    left = lane[:8] < ROWS
    moved = pltpu.roll(ahead, ROWS, 1)
    same = jnp.where(first, present, jnp.where(left, ahead, moved))
    beyond = jnp.where(first == left, ahead, moved)
    factor = factor_ref[...]
    for a, added in enumerate((upright, turned)):
        rows = slice(a * ROWS, (a + 1) * ROWS)
        tile = here[rows] + added + jnp.where(first, own[rows], 0.0)
        near_sum, far_sum = (
            jnp.where(left[:1], sums[a : a + 1], sums[2 + a : 3 + a]) for sums in (same, beyond)
        )
        far = jnp.where(below, far_sum, near_sum)
        tile = jnp.where(factor[rows] > 0.0, tile * factor[rows] / far, 0.0)
        swapped = pltpu.roll(tile, ROWS, 1)
        for group, twice in enumerate((jnp.where(lane < ROWS, tile, swapped), jnp.where(lane < ROWS, swapped, tile))):
            blocks = [pltpu.roll(twice[t : t + 8], 2 * ROWS - t, 1) if t else twice[:8] for t in range(0, ROWS, 8)]
            twice = jnp.concatenate(blocks, axis=0)
            for bit in range(3):
                moved = pltpu.roll(twice, 2 * ROWS - (1 << bit), 1)
                twice = jnp.where((row >> bit) & 1 == 1, moved, twice)
            out_ref[0, 2 * group + a] = twice[:, :ROWS]


def final_part(factor, own, kept, messages):
    vmem = pl.BlockSpec(memory_space=pltpu.VMEM)
    return pl.pallas_call(
        final_kernel,
        in_specs=[vmem] * (3 + len(messages)),
        out_specs=vmem,
        out_shape=jax.ShapeDtypeStruct((1, RADII, ROWS, ROWS), jnp.float32),
        compiler_params=pltpu.CompilerParams(vmem_limit_bytes=8 << 20),
        name="normalise_and_skew",
    )(factor, own, kept, *messages)


def factors(own, lag_width):
    tm, pix = lax.axis_index("tm"), lax.axis_index("pix")
    devices = lax.axis_size("tm")
    t = lax.broadcasted_iota(jnp.int32, (RADII, ROWS, ROWS), 1)
    s = lax.broadcasted_iota(jnp.int32, (RADII, ROWS, ROWS), 2)
    lag = jnp.where(s >= t, s - t, s - t + ROWS) + pix * ROWS
    valid = (lag < lag_width[0][:, None, None]) & (tm * ROWS + t + lag < devices * ROWS)
    annulus_size = PIX // RADII
    result = jnp.where(valid, annulus_size / own[:, :, None], 0.0)
    return packed(result.reshape(RADII * ROWS, ROWS))


def shards(frames, annulus_label, lag_width):
    devices = lax.axis_size("tm")
    pixels = frames.shape[2]
    pb, pix = lax.axis_index("pb"), lax.axis_index("pix")

    def far_pairs():
        for i in range(devices):
            for band, target in ((0, i - 2), (1, i + 2)):
                inside = 0 <= target < devices
                yield 2 * i + band, 2 * (target if inside else i) + (band if inside else 1 - band)

    def near_pairs():
        for i in range(devices):
            yield 2 * i + (1 - i % 2), 2 * (i ^ 1) + (1 - i % 2)
            yield 2 * i + i % 2, 2 * i + (1 - i % 2)

    tm_pb = ("tm", "pb")

    def sent(piece):
        near = lax.ppermute(piece, tm_pb, list(near_pairs()))
        return lax.ppermute(piece, tm_pb, list(far_pairs())), near

    unit = pixels // UNITS
    starts = [sum(SIZES[:index]) * unit for index in range(len(SIZES))]
    pieces = [lax.slice_in_dim(frames, 0, SIZES[0] * unit, axis=2), *later_pieces(frames, starts[1:])]
    own, third = own_part(annulus_label, pieces)
    received = [sent(piece) for piece in pieces]
    own, _ = lax.optimization_barrier((own, received[0]))
    own = own + lax.ppermute(own, "pix", [(0, 1), (1, 0)])
    factor = factors(own[2 * ROWS : 2 * ROWS + RADII, :ROWS], lag_width)

    pieces[2] = third
    states = []
    for index, (piece, (far, near)) in enumerate(zip(pieces, received)):
        last = index == len(SIZES) - 1
        before = states[-1] if states else None
        awaited = own
        if index == 0:
            awaited = far[:, :8, :128]
        result = chunk_part(piece, annulus_label, starts[index], far, near, before, awaited, last)
        states.append(result if last else result[0])
    state = states[-1]
    here_same, here_other, after_same, after_other = state

    def swapped(message, flip):
        pairs = [
            (i * 2 + x, (i ^ 1) * 2 + (x ^ flip)) for i in range(devices) for x in range(2) if i ^ 1 < devices
        ]
        return lax.ppermute(message, ("tm", "pix"), pairs)

    beside = lax.ppermute(here_other, "pix", [(0, 1), (1, 0)])
    after = [swapped(after_same, 0), swapped(after_other, 1)]
    here = here_same + beside
    handed = lax.ppermute(here, tm_pb, [(source ^ 1, target ^ 1) for source, target in far_pairs()])
    return final_part(factor, own, here, [handed, *after])


def solution(mesh):
    return jax.shard_map(
        shards,
        mesh=mesh,
        in_specs=(P("pb", "tm", "pix"), P("pb", "pix"), P("pb", None)),
        out_specs=P("pb", None, "tm", "pix"),
        check_vma=False,
    )
```

```python
import functools

import jax
import jax.numpy as jnp
from jax import lax
from jax.experimental import pallas as pl
from jax.experimental.pallas import tpu as pltpu
from jax.sharding import PartitionSpec as P

DELAYS_STORED = 128
PIX = 65536
RADII = 4
ROWS = 64
UNITS = 16
SIZES = (3, 9, 3, 1)
STRIP = 2048
NT = (((1,), (1,)), ((), ()))


def place():
    band = lax.axis_index("pb")
    return band, lax.axis_index("pix") == 1, lax.rem(lax.axis_index("tm"), 2) == band


def packed(tile):
    half = tile.shape[0] // 2
    return jnp.concatenate([tile[:half], tile[half:]], axis=1)


def masked_by_annulus(block, label):
    return [block * (label == a).astype(block.dtype) for a in range(RADII)]


def annulus_rows(label):
    ids = lax.broadcasted_iota(jnp.int32, (16, label.shape[1]), 0)
    return (label == ids).astype(jnp.float32).astype(jnp.bfloat16)


def products(rows, columns):
    return lax.dot_general(
        jnp.concatenate(rows, axis=0), columns, NT, preferred_element_type=jnp.float32
    )


def strips(size):
    return [(begin, min(begin + STRIP, size)) for begin in range(0, size, STRIP)]


def later_kernel(starts, frames_ref, *refs):
    count = len(starts)
    piece_refs, stage_refs, (in_semaphore, out_semaphore) = refs[:count], refs[count : 2 * count], refs[2 * count :]
    reads, writes = [], []
    for index, (start, piece_ref, stage_ref) in enumerate(zip(starts, piece_refs, stage_refs)):
        source = frames_ref.at[:, :, start : start + piece_ref.shape[2]]
        reads.append(pltpu.make_async_copy(source, stage_ref, in_semaphore.at[index]))
        writes.append(pltpu.make_async_copy(stage_ref, piece_ref, out_semaphore.at[index]))
    for read in reads:
        read.start()
    for read, write in zip(reads, writes):
        read.wait()
        write.start()
    for write in writes:
        write.wait()


def later_pieces(frames, starts):
    unit = frames.shape[2] // UNITS
    shapes = [(1, ROWS, count * unit) for count in SIZES[1:]]
    semaphores = pltpu.SemaphoreType.DMA((len(shapes),))
    return pl.pallas_call(
        functools.partial(later_kernel, starts),
        in_specs=[pl.BlockSpec(memory_space=pl.ANY)],
        out_specs=[pl.BlockSpec(memory_space=pl.ANY)] * len(shapes),
        out_shape=[jax.ShapeDtypeStruct(shape, frames.dtype) for shape in shapes],
        scratch_shapes=[pltpu.VMEM(shape, frames.dtype) for shape in shapes] + [semaphores] * 2,
        compiler_params=pltpu.CompilerParams(vmem_limit_bytes=60 << 20),
        name="later_pieces",
    )(frames)


def own_kernel(label_ref, *refs):
    *piece_refs, out_ref, copy_ref = refs
    copy_ref[...] = piece_refs[2][...]
    half = RADII * ROWS
    total, offset = None, 0
    for piece_ref in piece_refs:
        size = piece_ref.shape[2]
        for begin, end in strips(size):
            block = piece_ref[0, :, begin:end]
            label = label_ref[:, offset + begin : offset + end]
            part = products(masked_by_annulus(block, label) + [annulus_rows(label)], block)
            total = part if total is None else total + part
        offset += size
    tile, sums = total[:half], total[half : half + 8]
    t = lax.rem(lax.broadcasted_iota(jnp.int32, tile.shape, 0), ROWS)
    below = lax.broadcasted_iota(jnp.int32, tile.shape, 1) < t
    out_ref[: 2 * ROWS] = packed(jnp.where(below, 0.0, tile))
    out_ref[2 * ROWS :] = jnp.concatenate([sums, sums], axis=1)


def cost(pixels, rows, columns):
    return pl.CostEstimate(
        flops=2 * rows * columns * pixels, bytes_accessed=2 * columns * pixels, transcendentals=0
    )


def own_part(label, pieces):
    vmem = pl.BlockSpec(memory_space=pltpu.VMEM)
    return pl.pallas_call(
        own_kernel,
        in_specs=[vmem] * (1 + len(pieces)),
        out_specs=[vmem] * 2,
        out_shape=[
            jax.ShapeDtypeStruct((2 * ROWS + 8, 2 * ROWS), jnp.float32),
            jax.ShapeDtypeStruct(pieces[2].shape, pieces[2].dtype),
        ],
        compiler_params=pltpu.CompilerParams(vmem_limit_bytes=8 << 20),
        cost_estimate=cost(label.shape[1], 512, 256),
        name="own_tile_and_sums",
    )(label, *pieces)


def chunk_kernel(start, first, last, own_ref, label_ref, far_ref, near_ref, *refs):
    if not first:
        before_ref, *refs = refs
    if last:
        *out_refs, acc = refs
    else:
        _, acc = refs
    half = RADII * ROWS
    band, second, has_near = place()
    later = band == 1
    pieces = strips(near_ref.shape[2])

    def add(with_near):
        total = None
        for begin, end in pieces:
            own, near, far = (ref[0, :, begin:end] for ref in (own_ref, near_ref, far_ref))
            earliest = jnp.where(later, far, own)
            latest = jnp.where(later, own, far)
            label = label_ref[:, start + begin : start + end]
            rows = [annulus_rows(label)] + masked_by_annulus(earliest, label)
            if with_near:
                rows += masked_by_annulus(near, label)
            else:
                near = jnp.zeros_like(near)
            part = products(rows, jnp.concatenate([near, latest], axis=0))
            total = part if total is None else total + part
        count = total.shape[0]
        acc[:count] = total if first else total + before_ref[:count]
        if not with_near:
            acc[count:] = jnp.zeros_like(acc[count:])

    @pl.when(has_near)
    def _():
        add(True)

    @pl.when(jnp.logical_not(has_near))
    def _():
        add(False)

    if not last:
        return
    shape = (half, ROWS)
    t = lax.rem(lax.broadcasted_iota(jnp.int32, shape, 0), ROWS)
    below = lax.broadcasted_iota(jnp.int32, shape, 1) < t
    near_tile = acc[16 : 16 + half, :ROWS]
    far_tile = acc[16 : 16 + half, ROWS:]
    next_tile = acc[16 + half :, ROWS:]
    here = (jnp.where(below, near_tile, 0.0), jnp.where(below, far_tile, near_tile))
    sums = acc[:8]
    for ref, part in zip(out_refs[:2], (here, here[::-1])):
        ref[: 2 * ROWS] = packed(jnp.where(second, part[1], part[0]))
        ref[2 * ROWS :] = sums

    row = lax.broadcasted_iota(jnp.int32, (ROWS, 2 * ROWS), 0)
    lane = lax.broadcasted_iota(jnp.int32, (ROWS, 2 * ROWS), 1)
    column = lax.rem(lane, ROWS)
    tiles = packed(next_tile)
    upright = tiles[:ROWS]
    turned = tiles.T
    turned = jnp.where(lane < ROWS, pltpu.roll(turned[:ROWS], ROWS, 1), turned[ROWS:])
    low = jnp.where(column < row, upright, turned)
    high = jnp.where(column < row, turned, upright)
    diagonal = jnp.sum(jnp.where(column == row, turned, 0.0), axis=0, keepdims=True)
    beside = (lane[:8] < ROWS) & has_near
    after_sums = jnp.where(beside, pltpu.roll(sums, ROWS, 1), 0.0)
    after_sums = jnp.where(row[:8] == RADII, diagonal, after_sums)
    for ref, part in zip(out_refs[2:], ((low, high), (high, low))):
        ref[:ROWS] = jnp.where(second, part[1], part[0])
        ref[ROWS:] = after_sums


def chunk_part(piece, label, start, far, near, before, awaited, last):
    size = piece.shape[2]
    acc_shape = (16 + 2 * RADII * ROWS, 2 * ROWS)
    here, after = (2 * ROWS + 8, 2 * ROWS), (ROWS + 8, 2 * ROWS)
    vmem = pl.BlockSpec(memory_space=pltpu.VMEM)
    operands = [piece, label, far, near] + ([] if before is None else [before])
    if not last:
        operands.append(awaited)
    shapes = [here, here, after, after] if last else [acc_shape]
    return pl.pallas_call(
        functools.partial(chunk_kernel, start, before is None, last),
        in_specs=[vmem] * len(operands),
        out_specs=[vmem] * len(shapes),
        out_shape=[jax.ShapeDtypeStruct(shape, jnp.float32) for shape in shapes],
        scratch_shapes=[pltpu.VMEM(acc_shape, jnp.float32)] if last else [],
        compiler_params=pltpu.CompilerParams(vmem_limit_bytes=8 << 20),
        cost_estimate=cost(size if before is not None else 20 * size, 1024, 256),
        name="chunk_tiles",
    )(*operands)


def final_kernel(factor_ref, own_ref, kept_ref, here_ref, same_ref, other_ref, out_ref):
    band, second, _ = place()
    first = jnp.logical_not(second)
    inside = lax.axis_index("tm") < lax.axis_size("tm") - 2
    here = jnp.where(band == 0, kept_ref[...], jnp.where(inside, here_ref[...], 0.0))
    after = same_ref[...] + other_ref[...]
    own = own_ref[...]
    row = lax.broadcasted_iota(jnp.int32, (ROWS, 2 * ROWS), 0)
    lane = lax.broadcasted_iota(jnp.int32, (ROWS, 2 * ROWS), 1)
    column = lax.rem(lane, ROWS)
    below, above = column < row, column > row

    body = after[:ROWS]
    upright = jnp.where(below == first, body, 0.0)
    diagonal = jnp.where(column == row, after[ROWS + RADII : ROWS + RADII + 1], 0.0)
    turned = jnp.where(first, jnp.where(above, body, 0.0), jnp.where(below, body, diagonal))
    turned = jnp.concatenate([turned, turned], axis=0).T
    turned = jnp.where(lane < ROWS, turned[:ROWS], pltpu.roll(turned[ROWS:], ROWS, 1))

    ahead, present = here[2 * ROWS :] + after[ROWS:], own[2 * ROWS :]
    left = lane[:8] < ROWS
    moved = pltpu.roll(ahead, ROWS, 1)
    same = jnp.where(first, present, jnp.where(left, ahead, moved))
    beyond = jnp.where(first == left, ahead, moved)
    factor = factor_ref[...]
    for a, added in enumerate((upright, turned)):
        rows = slice(a * ROWS, (a + 1) * ROWS)
        tile = here[rows] + added + jnp.where(first, own[rows], 0.0)
        near_sum, far_sum = (
            jnp.where(left[:1], sums[a : a + 1], sums[2 + a : 3 + a]) for sums in (same, beyond)
        )
        far = jnp.where(below, far_sum, near_sum)
        tile = jnp.where(factor[rows] > 0.0, tile * factor[rows] / far, 0.0)
        swapped = pltpu.roll(tile, ROWS, 1)
        for group, twice in enumerate((jnp.where(lane < ROWS, tile, swapped), jnp.where(lane < ROWS, swapped, tile))):
            blocks = [pltpu.roll(twice[t : t + 8], 2 * ROWS - t, 1) if t else twice[:8] for t in range(0, ROWS, 8)]
            twice = jnp.concatenate(blocks, axis=0)
            for bit in range(3):
                moved = pltpu.roll(twice, 2 * ROWS - (1 << bit), 1)
                twice = jnp.where((row >> bit) & 1 == 1, moved, twice)
            out_ref[0, 2 * group + a] = twice[:, :ROWS]


def final_part(factor, own, kept, messages):
    vmem = pl.BlockSpec(memory_space=pltpu.VMEM)
    return pl.pallas_call(
        final_kernel,
        in_specs=[vmem] * (3 + len(messages)),
        out_specs=vmem,
        out_shape=jax.ShapeDtypeStruct((1, RADII, ROWS, ROWS), jnp.float32),
        compiler_params=pltpu.CompilerParams(vmem_limit_bytes=8 << 20),
        name="normalise_and_skew",
    )(factor, own, kept, *messages)


def factors(own, lag_width):
    tm, pix = lax.axis_index("tm"), lax.axis_index("pix")
    devices = lax.axis_size("tm")
    t = lax.broadcasted_iota(jnp.int32, (RADII, ROWS, ROWS), 1)
    s = lax.broadcasted_iota(jnp.int32, (RADII, ROWS, ROWS), 2)
    lag = jnp.where(s >= t, s - t, s - t + ROWS) + pix * ROWS
    valid = (lag < lag_width[0][:, None, None]) & (tm * ROWS + t + lag < devices * ROWS)
    annulus_size = PIX // RADII
    result = jnp.where(valid, annulus_size / own[:, :, None], 0.0)
    return packed(result.reshape(RADII * ROWS, ROWS))


def shards(frames, annulus_label, lag_width):
    devices = lax.axis_size("tm")
    pixels = frames.shape[2]
    pb, pix = lax.axis_index("pb"), lax.axis_index("pix")

    def far_pairs():
        for i in range(devices):
            for band, target in ((0, i - 2), (1, i + 2)):
                inside = 0 <= target < devices
                yield 2 * i + band, 2 * (target if inside else i) + (band if inside else 1 - band)

    def near_pairs():
        for i in range(devices):
            yield 2 * i + (1 - i % 2), 2 * (i ^ 1) + (1 - i % 2)
            yield 2 * i + i % 2, 2 * i + (1 - i % 2)

    tm_pb = ("tm", "pb")

    def sent(piece):
        near = lax.ppermute(piece, tm_pb, list(near_pairs()))
        return lax.ppermute(piece, tm_pb, list(far_pairs())), near

    unit = pixels // UNITS
    starts = [sum(SIZES[:index]) * unit for index in range(len(SIZES))]
    pieces = [lax.slice_in_dim(frames, 0, SIZES[0] * unit, axis=2), *later_pieces(frames, starts[1:])]
    own, third = own_part(annulus_label, pieces)
    received = [sent(piece) for piece in pieces]
    own, _ = lax.optimization_barrier((own, received[0]))
    own = own + lax.ppermute(own, "pix", [(0, 1), (1, 0)])
    factor = factors(own[2 * ROWS : 2 * ROWS + RADII, :ROWS], lag_width)

    pieces[2] = third
    states = []
    for index, (piece, (far, near)) in enumerate(zip(pieces, received)):
        last = index == len(SIZES) - 1
        before = states[-1] if states else None
        awaited = own
        if index == 0:
            awaited = far[:, :8, :128]
        result = chunk_part(piece, annulus_label, starts[index], far, near, before, awaited, last)
        states.append(result if last else result[0])
    state = states[-1]
    here_same, here_other, after_same, after_other = state

    def swapped(message, flip):
        pairs = [
            (i * 2 + x, (i ^ 1) * 2 + (x ^ flip)) for i in range(devices) for x in range(2) if i ^ 1 < devices
        ]
        return lax.ppermute(message, ("tm", "pix"), pairs)

    beside = lax.ppermute(here_other, "pix", [(0, 1), (1, 0)])
    after = [swapped(after_same, 0), swapped(after_other, 1)]
    here = here_same + beside
    handed = lax.ppermute(here, tm_pb, [(source ^ 1, target ^ 1) for source, target in far_pairs()])
    return final_part(factor, own, here, [handed, *after])


def solution(mesh):
    return jax.shard_map(
        shards,
        mesh=mesh,
        in_specs=(P("pb", "tm", "pix"), P("pb", "pix"), P("pb", None)),
        out_specs=P("pb", None, "tm", "pix"),
        check_vma=False,
    )
```

```python
import functools

import jax
import jax.numpy as jnp
from jax import lax
from jax.experimental import pallas as pl
from jax.experimental.pallas import tpu as pltpu
from jax.sharding import PartitionSpec as P

DELAYS_STORED = 128
PIX = 65536
RADII = 4
ROWS = 64
UNITS = 16
SIZES = (3, 9, 3, 1)
STRIP = 2048
NT = (((1,), (1,)), ((), ()))


def place():
    band = lax.axis_index("pb")
    return band, lax.axis_index("pix") == 1, lax.rem(lax.axis_index("tm"), 2) == band


def packed(tile):
    half = tile.shape[0] // 2
    return jnp.concatenate([tile[:half], tile[half:]], axis=1)


def masked_by_annulus(block, label):
    return [block * (label == a).astype(block.dtype) for a in range(RADII)]


def annulus_rows(label):
    ids = lax.broadcasted_iota(jnp.int32, (16, label.shape[1]), 0)
    return (label == ids).astype(jnp.float32).astype(jnp.bfloat16)


def products(rows, columns):
    return lax.dot_general(
        jnp.concatenate(rows, axis=0), columns, NT, preferred_element_type=jnp.float32
    )


def strips(size):
    return [(begin, min(begin + STRIP, size)) for begin in range(0, size, STRIP)]


def later_kernel(starts, frames_ref, *refs):
    count = len(starts)
    piece_refs, stage_refs, (in_semaphore, out_semaphore) = refs[:count], refs[count : 2 * count], refs[2 * count :]
    reads, writes = [], []
    for index, (start, piece_ref, stage_ref) in enumerate(zip(starts, piece_refs, stage_refs)):
        source = frames_ref.at[:, :, start : start + piece_ref.shape[2]]
        reads.append(pltpu.make_async_copy(source, stage_ref, in_semaphore.at[index]))
        writes.append(pltpu.make_async_copy(stage_ref, piece_ref, out_semaphore.at[index]))
    for read in reads:
        read.start()
    for read, write in zip(reads, writes):
        read.wait()
        write.start()
    for write in writes:
        write.wait()


def later_pieces(frames, starts):
    unit = frames.shape[2] // UNITS
    shapes = [(1, ROWS, count * unit) for count in SIZES[1:]]
    semaphores = pltpu.SemaphoreType.DMA((len(shapes),))
    return pl.pallas_call(
        functools.partial(later_kernel, starts),
        in_specs=[pl.BlockSpec(memory_space=pl.ANY)],
        out_specs=[pl.BlockSpec(memory_space=pl.ANY)] * len(shapes),
        out_shape=[jax.ShapeDtypeStruct(shape, frames.dtype) for shape in shapes],
        scratch_shapes=[pltpu.VMEM(shape, frames.dtype) for shape in shapes] + [semaphores] * 2,
        compiler_params=pltpu.CompilerParams(vmem_limit_bytes=60 << 20),
        name="later_pieces",
    )(frames)


def own_kernel(label_ref, *refs):
    *piece_refs, out_ref, copy_ref = refs
    copy_ref[...] = piece_refs[2][...]
    half = RADII * ROWS
    total, offset = None, 0
    for piece_ref in piece_refs:
        size = piece_ref.shape[2]
        for begin, end in strips(size):
            block = piece_ref[0, :, begin:end]
            label = label_ref[:, offset + begin : offset + end]
            part = products(masked_by_annulus(block, label) + [annulus_rows(label)], block)
            total = part if total is None else total + part
        offset += size
    tile, sums = total[:half], total[half : half + 8]
    t = lax.rem(lax.broadcasted_iota(jnp.int32, tile.shape, 0), ROWS)
    below = lax.broadcasted_iota(jnp.int32, tile.shape, 1) < t
    out_ref[: 2 * ROWS] = packed(jnp.where(below, 0.0, tile))
    out_ref[2 * ROWS :] = jnp.concatenate([sums, sums], axis=1)


def cost(pixels, rows, columns):
    return pl.CostEstimate(
        flops=2 * rows * columns * pixels, bytes_accessed=2 * columns * pixels, transcendentals=0
    )


def own_part(label, pieces):
    vmem = pl.BlockSpec(memory_space=pltpu.VMEM)
    return pl.pallas_call(
        own_kernel,
        in_specs=[vmem] * (1 + len(pieces)),
        out_specs=[vmem] * 2,
        out_shape=[
            jax.ShapeDtypeStruct((2 * ROWS + 8, 2 * ROWS), jnp.float32),
            jax.ShapeDtypeStruct(pieces[2].shape, pieces[2].dtype),
        ],
        compiler_params=pltpu.CompilerParams(vmem_limit_bytes=8 << 20),
        cost_estimate=cost(label.shape[1], 512, 256),
        name="own_tile_and_sums",
    )(label, *pieces)


def chunk_kernel(start, first, last, own_ref, label_ref, far_ref, near_ref, *refs):
    if not first:
        before_ref, *refs = refs
    if last:
        *out_refs, acc = refs
    else:
        _, acc = refs
    half = RADII * ROWS
    band, second, has_near = place()
    later = band == 1
    pieces = strips(near_ref.shape[2])

    def add(with_near):
        total = None
        for begin, end in pieces:
            own, near, far = (ref[0, :, begin:end] for ref in (own_ref, near_ref, far_ref))
            earliest = jnp.where(later, far, own)
            latest = jnp.where(later, own, far)
            label = label_ref[:, start + begin : start + end]
            rows = [annulus_rows(label)] + masked_by_annulus(earliest, label)
            if with_near:
                rows += masked_by_annulus(near, label)
            else:
                near = jnp.zeros_like(near)
            part = products(rows, jnp.concatenate([near, latest], axis=0))
            total = part if total is None else total + part
        count = total.shape[0]
        acc[:count] = total if first else total + before_ref[:count]
        if not with_near:
            acc[count:] = jnp.zeros_like(acc[count:])

    @pl.when(has_near)
    def _():
        add(True)

    @pl.when(jnp.logical_not(has_near))
    def _():
        add(False)

    if not last:
        return
    shape = (half, ROWS)
    t = lax.rem(lax.broadcasted_iota(jnp.int32, shape, 0), ROWS)
    below = lax.broadcasted_iota(jnp.int32, shape, 1) < t
    near_tile = acc[16 : 16 + half, :ROWS]
    far_tile = acc[16 : 16 + half, ROWS:]
    next_tile = acc[16 + half :, ROWS:]
    here = (jnp.where(below, near_tile, 0.0), jnp.where(below, far_tile, near_tile))
    sums = acc[:8]
    for ref, part in zip(out_refs[:2], (here, here[::-1])):
        ref[: 2 * ROWS] = packed(jnp.where(second, part[1], part[0]))
        ref[2 * ROWS :] = sums

    row = lax.broadcasted_iota(jnp.int32, (ROWS, 2 * ROWS), 0)
    lane = lax.broadcasted_iota(jnp.int32, (ROWS, 2 * ROWS), 1)
    column = lax.rem(lane, ROWS)
    tiles = packed(next_tile)
    upright = tiles[:ROWS]
    turned = tiles.T
    turned = jnp.where(lane < ROWS, pltpu.roll(turned[:ROWS], ROWS, 1), turned[ROWS:])
    low = jnp.where(column < row, upright, turned)
    high = jnp.where(column < row, turned, upright)
    diagonal = jnp.sum(jnp.where(column == row, turned, 0.0), axis=0, keepdims=True)
    beside = (lane[:8] < ROWS) & has_near
    after_sums = jnp.where(beside, pltpu.roll(sums, ROWS, 1), 0.0)
    after_sums = jnp.where(row[:8] == RADII, diagonal, after_sums)
    for ref, part in zip(out_refs[2:], ((low, high), (high, low))):
        ref[:ROWS] = jnp.where(second, part[1], part[0])
        ref[ROWS:] = after_sums


def chunk_part(piece, label, start, far, near, before, awaited, last):
    size = piece.shape[2]
    acc_shape = (16 + 2 * RADII * ROWS, 2 * ROWS)
    here, after = (2 * ROWS + 8, 2 * ROWS), (ROWS + 8, 2 * ROWS)
    vmem = pl.BlockSpec(memory_space=pltpu.VMEM)
    operands = [piece, label, far, near] + ([] if before is None else [before])
    if not last:
        operands.append(awaited)
    shapes = [here, here, after, after] if last else [acc_shape]
    return pl.pallas_call(
        functools.partial(chunk_kernel, start, before is None, last),
        in_specs=[vmem] * len(operands),
        out_specs=[vmem] * len(shapes),
        out_shape=[jax.ShapeDtypeStruct(shape, jnp.float32) for shape in shapes],
        scratch_shapes=[pltpu.VMEM(acc_shape, jnp.float32)] if last else [],
        compiler_params=pltpu.CompilerParams(vmem_limit_bytes=8 << 20),
        cost_estimate=cost(size if before is not None else 20 * size, 1024, 256),
        name="chunk_tiles",
    )(*operands)


def final_kernel(factor_ref, own_ref, kept_ref, here_ref, same_ref, other_ref, out_ref):
    band, second, _ = place()
    first = jnp.logical_not(second)
    inside = lax.axis_index("tm") < lax.axis_size("tm") - 2
    here = jnp.where(band == 0, kept_ref[...], jnp.where(inside, here_ref[...], 0.0))
    after = same_ref[...] + other_ref[...]
    own = own_ref[...]
    row = lax.broadcasted_iota(jnp.int32, (ROWS, 2 * ROWS), 0)
    lane = lax.broadcasted_iota(jnp.int32, (ROWS, 2 * ROWS), 1)
    column = lax.rem(lane, ROWS)
    below, above = column < row, column > row

    body = after[:ROWS]
    upright = jnp.where(below == first, body, 0.0)
    diagonal = jnp.where(column == row, after[ROWS + RADII : ROWS + RADII + 1], 0.0)
    turned = jnp.where(first, jnp.where(above, body, 0.0), jnp.where(below, body, diagonal))
    turned = jnp.concatenate([turned, turned], axis=0).T
    turned = jnp.where(lane < ROWS, turned[:ROWS], pltpu.roll(turned[ROWS:], ROWS, 1))

    ahead, present = here[2 * ROWS :] + after[ROWS:], own[2 * ROWS :]
    left = lane[:8] < ROWS
    moved = pltpu.roll(ahead, ROWS, 1)
    same = jnp.where(first, present, jnp.where(left, ahead, moved))
    beyond = jnp.where(first == left, ahead, moved)
    factor = factor_ref[...]
    for a, added in enumerate((upright, turned)):
        rows = slice(a * ROWS, (a + 1) * ROWS)
        tile = here[rows] + added + jnp.where(first, own[rows], 0.0)
        near_sum, far_sum = (
            jnp.where(left[:1], sums[a : a + 1], sums[2 + a : 3 + a]) for sums in (same, beyond)
        )
        far = jnp.where(below, far_sum, near_sum)
        tile = jnp.where(factor[rows] > 0.0, tile * factor[rows] / far, 0.0)
        swapped = pltpu.roll(tile, ROWS, 1)
        for group, twice in enumerate((jnp.where(lane < ROWS, tile, swapped), jnp.where(lane < ROWS, swapped, tile))):
            blocks = [pltpu.roll(twice[t : t + 8], 2 * ROWS - t, 1) if t else twice[:8] for t in range(0, ROWS, 8)]
            twice = jnp.concatenate(blocks, axis=0)
            for bit in range(3):
                moved = pltpu.roll(twice, 2 * ROWS - (1 << bit), 1)
                twice = jnp.where((row >> bit) & 1 == 1, moved, twice)
            out_ref[0, 2 * group + a] = twice[:, :ROWS]


def final_part(factor, own, kept, messages):
    vmem = pl.BlockSpec(memory_space=pltpu.VMEM)
    return pl.pallas_call(
        final_kernel,
        in_specs=[vmem] * (3 + len(messages)),
        out_specs=vmem,
        out_shape=jax.ShapeDtypeStruct((1, RADII, ROWS, ROWS), jnp.float32),
        compiler_params=pltpu.CompilerParams(vmem_limit_bytes=8 << 20),
        name="normalise_and_skew",
    )(factor, own, kept, *messages)


def factors(own, lag_width):
    tm, pix = lax.axis_index("tm"), lax.axis_index("pix")
    devices = lax.axis_size("tm")
    t = lax.broadcasted_iota(jnp.int32, (RADII, ROWS, ROWS), 1)
    s = lax.broadcasted_iota(jnp.int32, (RADII, ROWS, ROWS), 2)
    lag = jnp.where(s >= t, s - t, s - t + ROWS) + pix * ROWS
    valid = (lag < lag_width[0][:, None, None]) & (tm * ROWS + t + lag < devices * ROWS)
    annulus_size = PIX // RADII
    result = jnp.where(valid, annulus_size / own[:, :, None], 0.0)
    return packed(result.reshape(RADII * ROWS, ROWS))


def shards(frames, annulus_label, lag_width):
    devices = lax.axis_size("tm")
    pixels = frames.shape[2]
    pb, pix = lax.axis_index("pb"), lax.axis_index("pix")

    def far_pairs():
        for i in range(devices):
            for band, target in ((0, i - 2), (1, i + 2)):
                inside = 0 <= target < devices
                yield 2 * i + band, 2 * (target if inside else i) + (band if inside else 1 - band)

    def near_pairs():
        for i in range(devices):
            yield 2 * i + (1 - i % 2), 2 * (i ^ 1) + (1 - i % 2)
            yield 2 * i + i % 2, 2 * i + (1 - i % 2)

    tm_pb = ("tm", "pb")

    def sent(piece):
        near = lax.ppermute(piece, tm_pb, list(near_pairs()))
        return lax.ppermute(piece, tm_pb, list(far_pairs())), near

    unit = pixels // UNITS
    starts = [sum(SIZES[:index]) * unit for index in range(len(SIZES))]
    pieces = [lax.slice_in_dim(frames, 0, SIZES[0] * unit, axis=2), *later_pieces(frames, starts[1:])]
    own, third = own_part(annulus_label, pieces)
    received = [sent(piece) for piece in pieces]
    own, _ = lax.optimization_barrier((own, received[0]))
    own = own + lax.ppermute(own, "pix", [(0, 1), (1, 0)])
    factor = factors(own[2 * ROWS : 2 * ROWS + RADII, :ROWS], lag_width)

    pieces[2] = third
    states = []
    for index, (piece, (far, near)) in enumerate(zip(pieces, received)):
        last = index == len(SIZES) - 1
        before = states[-1] if states else None
        awaited = own
        if index == 0:
            awaited = near[:, :8, :128]
        result = chunk_part(piece, annulus_label, starts[index], far, near, before, awaited, last)
        states.append(result if last else result[0])
    state = states[-1]
    here_same, here_other, after_same, after_other = state

    def swapped(message, flip):
        pairs = [
            (i * 2 + x, (i ^ 1) * 2 + (x ^ flip)) for i in range(devices) for x in range(2) if i ^ 1 < devices
        ]
        return lax.ppermute(message, ("tm", "pix"), pairs)

    beside = lax.ppermute(here_other, "pix", [(0, 1), (1, 0)])
    after = [swapped(after_same, 0), swapped(after_other, 1)]
    here = here_same + beside
    handed = lax.ppermute(here, tm_pb, [(source ^ 1, target ^ 1) for source, target in far_pairs()])
    return final_part(factor, own, here, [handed, *after])


def solution(mesh):
    return jax.shard_map(
        shards,
        mesh=mesh,
        in_specs=(P("pb", "tm", "pix"), P("pb", "pix"), P("pb", None)),
        out_specs=P("pb", None, "tm", "pix"),
        check_vma=False,
    )
```

```python
import functools

import jax
import jax.numpy as jnp
from jax import lax
from jax.experimental import pallas as pl
from jax.experimental.pallas import tpu as pltpu
from jax.sharding import PartitionSpec as P

DELAYS_STORED = 128
PIX = 65536
RADII = 4
ROWS = 64
UNITS = 16
SIZES = (3, 9, 3, 1)
STRIP = 1024
NT = (((1,), (1,)), ((), ()))


def place():
    band = lax.axis_index("pb")
    return band, lax.axis_index("pix") == 1, lax.rem(lax.axis_index("tm"), 2) == band


def packed(tile):
    half = tile.shape[0] // 2
    return jnp.concatenate([tile[:half], tile[half:]], axis=1)


def masked_by_annulus(block, label):
    return [block * (label == a).astype(block.dtype) for a in range(RADII)]


def annulus_rows(label):
    ids = lax.broadcasted_iota(jnp.int32, (16, label.shape[1]), 0)
    return (label == ids).astype(jnp.float32).astype(jnp.bfloat16)


def products(rows, columns):
    return lax.dot_general(
        jnp.concatenate(rows, axis=0), columns, NT, preferred_element_type=jnp.float32
    )


def strips(size):
    return [(begin, min(begin + STRIP, size)) for begin in range(0, size, STRIP)]


def later_kernel(starts, frames_ref, *refs):
    count = len(starts)
    piece_refs, stage_refs, (in_semaphore, out_semaphore) = refs[:count], refs[count : 2 * count], refs[2 * count :]
    reads, writes = [], []
    for index, (start, piece_ref, stage_ref) in enumerate(zip(starts, piece_refs, stage_refs)):
        source = frames_ref.at[:, :, start : start + piece_ref.shape[2]]
        reads.append(pltpu.make_async_copy(source, stage_ref, in_semaphore.at[index]))
        writes.append(pltpu.make_async_copy(stage_ref, piece_ref, out_semaphore.at[index]))
    for read in reads:
        read.start()
    for read, write in zip(reads, writes):
        read.wait()
        write.start()
    for write in writes:
        write.wait()


def later_pieces(frames, starts):
    unit = frames.shape[2] // UNITS
    shapes = [(1, ROWS, count * unit) for count in SIZES[1:]]
    semaphores = pltpu.SemaphoreType.DMA((len(shapes),))
    return pl.pallas_call(
        functools.partial(later_kernel, starts),
        in_specs=[pl.BlockSpec(memory_space=pl.ANY)],
        out_specs=[pl.BlockSpec(memory_space=pl.ANY)] * len(shapes),
        out_shape=[jax.ShapeDtypeStruct(shape, frames.dtype) for shape in shapes],
        scratch_shapes=[pltpu.VMEM(shape, frames.dtype) for shape in shapes] + [semaphores] * 2,
        compiler_params=pltpu.CompilerParams(vmem_limit_bytes=60 << 20),
        name="later_pieces",
    )(frames)


def own_kernel(label_ref, *refs):
    *piece_refs, out_ref, copy_ref = refs
    copy_ref[...] = piece_refs[2][...]
    half = RADII * ROWS
    total, offset = None, 0
    for piece_ref in piece_refs:
        size = piece_ref.shape[2]
        for begin, end in strips(size):
            block = piece_ref[0, :, begin:end]
            label = label_ref[:, offset + begin : offset + end]
            part = products(masked_by_annulus(block, label) + [annulus_rows(label)], block)
            total = part if total is None else total + part
        offset += size
    tile, sums = total[:half], total[half : half + 8]
    t = lax.rem(lax.broadcasted_iota(jnp.int32, tile.shape, 0), ROWS)
    below = lax.broadcasted_iota(jnp.int32, tile.shape, 1) < t
    out_ref[: 2 * ROWS] = packed(jnp.where(below, 0.0, tile))
    out_ref[2 * ROWS :] = jnp.concatenate([sums, sums], axis=1)


def cost(pixels, rows, columns):
    return pl.CostEstimate(
        flops=2 * rows * columns * pixels, bytes_accessed=2 * columns * pixels, transcendentals=0
    )


def own_part(label, pieces):
    vmem = pl.BlockSpec(memory_space=pltpu.VMEM)
    return pl.pallas_call(
        own_kernel,
        in_specs=[vmem] * (1 + len(pieces)),
        out_specs=[vmem] * 2,
        out_shape=[
            jax.ShapeDtypeStruct((2 * ROWS + 8, 2 * ROWS), jnp.float32),
            jax.ShapeDtypeStruct(pieces[2].shape, pieces[2].dtype),
        ],
        compiler_params=pltpu.CompilerParams(vmem_limit_bytes=8 << 20),
        cost_estimate=cost(label.shape[1], 512, 256),
        name="own_tile_and_sums",
    )(label, *pieces)


def chunk_kernel(start, first, last, own_ref, label_ref, far_ref, near_ref, *refs):
    if not first:
        before_ref, *refs = refs
    if last:
        *out_refs, acc = refs
    else:
        _, acc = refs
    half = RADII * ROWS
    band, second, has_near = place()
    later = band == 1
    pieces = strips(near_ref.shape[2])

    def add(with_near):
        total = None
        for begin, end in pieces:
            own, near, far = (ref[0, :, begin:end] for ref in (own_ref, near_ref, far_ref))
            earliest = jnp.where(later, far, own)
            latest = jnp.where(later, own, far)
            label = label_ref[:, start + begin : start + end]
            rows = [annulus_rows(label)] + masked_by_annulus(earliest, label)
            if with_near:
                rows += masked_by_annulus(near, label)
            else:
                near = jnp.zeros_like(near)
            part = products(rows, jnp.concatenate([near, latest], axis=0))
            total = part if total is None else total + part
        count = total.shape[0]
        acc[:count] = total if first else total + before_ref[:count]
        if not with_near:
            acc[count:] = jnp.zeros_like(acc[count:])

    @pl.when(has_near)
    def _():
        add(True)

    @pl.when(jnp.logical_not(has_near))
    def _():
        add(False)

    if not last:
        return
    shape = (half, ROWS)
    t = lax.rem(lax.broadcasted_iota(jnp.int32, shape, 0), ROWS)
    below = lax.broadcasted_iota(jnp.int32, shape, 1) < t
    near_tile = acc[16 : 16 + half, :ROWS]
    far_tile = acc[16 : 16 + half, ROWS:]
    next_tile = acc[16 + half :, ROWS:]
    here = (jnp.where(below, near_tile, 0.0), jnp.where(below, far_tile, near_tile))
    sums = acc[:8]
    for ref, part in zip(out_refs[:2], (here, here[::-1])):
        ref[: 2 * ROWS] = packed(jnp.where(second, part[1], part[0]))
        ref[2 * ROWS :] = sums

    row = lax.broadcasted_iota(jnp.int32, (ROWS, 2 * ROWS), 0)
    lane = lax.broadcasted_iota(jnp.int32, (ROWS, 2 * ROWS), 1)
    column = lax.rem(lane, ROWS)
    tiles = packed(next_tile)
    upright = tiles[:ROWS]
    turned = tiles.T
    turned = jnp.where(lane < ROWS, pltpu.roll(turned[:ROWS], ROWS, 1), turned[ROWS:])
    low = jnp.where(column < row, upright, turned)
    high = jnp.where(column < row, turned, upright)
    diagonal = jnp.sum(jnp.where(column == row, turned, 0.0), axis=0, keepdims=True)
    beside = (lane[:8] < ROWS) & has_near
    after_sums = jnp.where(beside, pltpu.roll(sums, ROWS, 1), 0.0)
    after_sums = jnp.where(row[:8] == RADII, diagonal, after_sums)
    for ref, part in zip(out_refs[2:], ((low, high), (high, low))):
        ref[:ROWS] = jnp.where(second, part[1], part[0])
        ref[ROWS:] = after_sums


def chunk_part(piece, label, start, far, near, before, awaited, last):
    size = piece.shape[2]
    acc_shape = (16 + 2 * RADII * ROWS, 2 * ROWS)
    here, after = (2 * ROWS + 8, 2 * ROWS), (ROWS + 8, 2 * ROWS)
    vmem = pl.BlockSpec(memory_space=pltpu.VMEM)
    operands = [piece, label, far, near] + ([] if before is None else [before])
    if not last:
        operands.append(awaited)
    shapes = [here, here, after, after] if last else [acc_shape]
    return pl.pallas_call(
        functools.partial(chunk_kernel, start, before is None, last),
        in_specs=[vmem] * len(operands),
        out_specs=[vmem] * len(shapes),
        out_shape=[jax.ShapeDtypeStruct(shape, jnp.float32) for shape in shapes],
        scratch_shapes=[pltpu.VMEM(acc_shape, jnp.float32)] if last else [],
        compiler_params=pltpu.CompilerParams(vmem_limit_bytes=8 << 20),
        cost_estimate=cost(size if before is not None else 20 * size, 1024, 256),
        name="chunk_tiles",
    )(*operands)


def final_kernel(factor_ref, own_ref, kept_ref, here_ref, same_ref, other_ref, out_ref):
    band, second, _ = place()
    first = jnp.logical_not(second)
    inside = lax.axis_index("tm") < lax.axis_size("tm") - 2
    here = jnp.where(band == 0, kept_ref[...], jnp.where(inside, here_ref[...], 0.0))
    after = same_ref[...] + other_ref[...]
    own = own_ref[...]
    row = lax.broadcasted_iota(jnp.int32, (ROWS, 2 * ROWS), 0)
    lane = lax.broadcasted_iota(jnp.int32, (ROWS, 2 * ROWS), 1)
    column = lax.rem(lane, ROWS)
    below, above = column < row, column > row

    body = after[:ROWS]
    upright = jnp.where(below == first, body, 0.0)
    diagonal = jnp.where(column == row, after[ROWS + RADII : ROWS + RADII + 1], 0.0)
    turned = jnp.where(first, jnp.where(above, body, 0.0), jnp.where(below, body, diagonal))
    turned = jnp.concatenate([turned, turned], axis=0).T
    turned = jnp.where(lane < ROWS, turned[:ROWS], pltpu.roll(turned[ROWS:], ROWS, 1))

    ahead, present = here[2 * ROWS :] + after[ROWS:], own[2 * ROWS :]
    left = lane[:8] < ROWS
    moved = pltpu.roll(ahead, ROWS, 1)
    same = jnp.where(first, present, jnp.where(left, ahead, moved))
    beyond = jnp.where(first == left, ahead, moved)
    factor = factor_ref[...]
    for a, added in enumerate((upright, turned)):
        rows = slice(a * ROWS, (a + 1) * ROWS)
        tile = here[rows] + added + jnp.where(first, own[rows], 0.0)
        near_sum, far_sum = (
            jnp.where(left[:1], sums[a : a + 1], sums[2 + a : 3 + a]) for sums in (same, beyond)
        )
        far = jnp.where(below, far_sum, near_sum)
        tile = jnp.where(factor[rows] > 0.0, tile * factor[rows] / far, 0.0)
        swapped = pltpu.roll(tile, ROWS, 1)
        for group, twice in enumerate((jnp.where(lane < ROWS, tile, swapped), jnp.where(lane < ROWS, swapped, tile))):
            blocks = [pltpu.roll(twice[t : t + 8], 2 * ROWS - t, 1) if t else twice[:8] for t in range(0, ROWS, 8)]
            twice = jnp.concatenate(blocks, axis=0)
            for bit in range(3):
                moved = pltpu.roll(twice, 2 * ROWS - (1 << bit), 1)
                twice = jnp.where((row >> bit) & 1 == 1, moved, twice)
            out_ref[0, 2 * group + a] = twice[:, :ROWS]


def final_part(factor, own, kept, messages):
    vmem = pl.BlockSpec(memory_space=pltpu.VMEM)
    return pl.pallas_call(
        final_kernel,
        in_specs=[vmem] * (3 + len(messages)),
        out_specs=vmem,
        out_shape=jax.ShapeDtypeStruct((1, RADII, ROWS, ROWS), jnp.float32),
        compiler_params=pltpu.CompilerParams(vmem_limit_bytes=8 << 20),
        name="normalise_and_skew",
    )(factor, own, kept, *messages)


def factors(own, lag_width):
    tm, pix = lax.axis_index("tm"), lax.axis_index("pix")
    devices = lax.axis_size("tm")
    t = lax.broadcasted_iota(jnp.int32, (RADII, ROWS, ROWS), 1)
    s = lax.broadcasted_iota(jnp.int32, (RADII, ROWS, ROWS), 2)
    lag = jnp.where(s >= t, s - t, s - t + ROWS) + pix * ROWS
    valid = (lag < lag_width[0][:, None, None]) & (tm * ROWS + t + lag < devices * ROWS)
    annulus_size = PIX // RADII
    result = jnp.where(valid, annulus_size / own[:, :, None], 0.0)
    return packed(result.reshape(RADII * ROWS, ROWS))


def shards(frames, annulus_label, lag_width):
    devices = lax.axis_size("tm")
    pixels = frames.shape[2]
    pb, pix = lax.axis_index("pb"), lax.axis_index("pix")

    def far_pairs():
        for i in range(devices):
            for band, target in ((0, i - 2), (1, i + 2)):
                inside = 0 <= target < devices
                yield 2 * i + band, 2 * (target if inside else i) + (band if inside else 1 - band)

    def near_pairs():
        for i in range(devices):
            yield 2 * i + (1 - i % 2), 2 * (i ^ 1) + (1 - i % 2)
            yield 2 * i + i % 2, 2 * i + (1 - i % 2)

    tm_pb = ("tm", "pb")

    def sent(piece):
        near = lax.ppermute(piece, tm_pb, list(near_pairs()))
        return lax.ppermute(piece, tm_pb, list(far_pairs())), near

    unit = pixels // UNITS
    starts = [sum(SIZES[:index]) * unit for index in range(len(SIZES))]
    pieces = [lax.slice_in_dim(frames, 0, SIZES[0] * unit, axis=2), *later_pieces(frames, starts[1:])]
    own, third = own_part(annulus_label, pieces)
    received = [sent(piece) for piece in pieces]
    own, _ = lax.optimization_barrier((own, received[0]))
    own = own + lax.ppermute(own, "pix", [(0, 1), (1, 0)])
    factor = factors(own[2 * ROWS : 2 * ROWS + RADII, :ROWS], lag_width)

    pieces[2] = third
    states = []
    for index, (piece, (far, near)) in enumerate(zip(pieces, received)):
        last = index == len(SIZES) - 1
        before = states[-1] if states else None
        awaited = own
        if index == 0:
            awaited = far[:, :8, :128]
        result = chunk_part(piece, annulus_label, starts[index], far, near, before, awaited, last)
        states.append(result if last else result[0])
    state = states[-1]
    here_same, here_other, after_same, after_other = state

    def swapped(message, flip):
        pairs = [
            (i * 2 + x, (i ^ 1) * 2 + (x ^ flip)) for i in range(devices) for x in range(2) if i ^ 1 < devices
        ]
        return lax.ppermute(message, ("tm", "pix"), pairs)

    beside = lax.ppermute(here_other, "pix", [(0, 1), (1, 0)])
    after = [swapped(after_same, 0), swapped(after_other, 1)]
    here = here_same + beside
    handed = lax.ppermute(here, tm_pb, [(source ^ 1, target ^ 1) for source, target in far_pairs()])
    return final_part(factor, own, here, [handed, *after])


def solution(mesh):
    return jax.shard_map(
        shards,
        mesh=mesh,
        in_specs=(P("pb", "tm", "pix"), P("pb", "pix"), P("pb", None)),
        out_specs=P("pb", None, "tm", "pix"),
        check_vma=False,
    )
```
